512 devices in a mesh: row: 32 (over x, y), col: 16 (over z, core).
Axes of the slice: x: 4, y: 8, z: 8, core: 2. Of those that a mesh axis runs over, the one named last changes fastest.
Arguments:
- eigvecs: float32 [65536, 2048], P('row', 'col'), may hold values from -6 to 6
- reflectors: float32 [16, 1024, 64], P('col', 'row'), may hold values from -5 to 5, as said below
Outputs:
- transformed: float32 [65536, 2048], P('row', 'col')
The draws below stay inside these ranges and needn't reach their ends.
Inputs may be any that keep to these rules, and one draw needn't show every extreme that they name: `reflectors`: entry 0 of every vector is 1; in sweep j, block k, entry i is 0 wherever j + k * 64 + i >= 65536.
All inputs are finite; a program needn't handle non-finite values.
Results may differ from the reference program's by a relative error of at most 0.00016.
Values sent between devices are 32-bit elements; how exact they have to be, the bound alone decides.
No kernel may reach another device: no remote copies, remote signals or barrier semaphores. Data moves between devices by JAX's collectives and lax.ppermute only.
A program may use at most 64 MiB of HBM per device.

```python
import jax
import jax.numpy as jnp
from jax import lax

B = 64
M = 2048
S = 16
NROWS = 65536


def draw_reflectors(key, part):
    key = jax.random.fold_in(key, 7)
    shape = (S, NROWS // B, B)
    values = jnp.clip(jax.random.normal(key, shape, jnp.float32), -5.0, 5.0)
    sweep_ids = lax.broadcasted_iota(jnp.int32, shape, 0)
    block_ids = lax.broadcasted_iota(jnp.int32, shape, 1)
    entry_ids = lax.broadcasted_iota(jnp.int32, shape, 2)
    inside = sweep_ids + block_ids * B + entry_ids < NROWS
    values = jnp.where(inside, values, jnp.zeros_like(values))
    values = jnp.where(entry_ids == 0, jnp.ones_like(values), values)
    return values.astype(jnp.float32)


def levels(key, extent, shards, smallest, largest):
    level = 1.0
    for axis_at, parts in shards:
        draws = jax.random.uniform(jax.random.fold_in(jax.random.fold_in(key, 6), axis_at), (parts,), jnp.float32, smallest / len(shards), largest / len(shards))
        level = level * jnp.repeat(jnp.exp(draws), extent[axis_at] // parts).reshape((-1,) + (1,) * (len(extent) - 1 - axis_at))
    return level


def gaussian(stream_key, shape, scale, reach, cuts=(), held_as=jnp.bfloat16):
    entries = scale * jax.random.normal(stream_key, shape, jnp.float32)
    if cuts:
        entries = entries * levels(stream_key, shape, cuts, -0.22, 0.18)
    return jnp.clip(entries, -reach, reach).astype(held_as)


def setup_inputs(seed: int = 0) -> dict:
    key_of = jax.random.split(jax.random.key(seed), 3)
    return {
        "eigvecs": gaussian(key_of[0], (NROWS, M), 1.0, 6.0, ((0, 32), (1, 16)), jnp.float32),
        "reflectors": draw_reflectors(jax.random.fold_in(key_of[2], 71), 0),
    }


def apply_blocks(vectors, segment):
    leading = jnp.where(lax.broadcasted_iota(jnp.int32, vectors.shape, 1) == 0, jnp.ones_like(vectors), vectors)
    scales = 2.0 / jnp.sum(leading * leading, axis=1)
    projected = jnp.einsum("kb,kbc->kc", leading, segment, precision=lax.Precision.HIGHEST)
    return segment - (leading * scales[:, None])[:, :, None] * projected[:, None, :]


def reference(eigvecs, reflectors):
    total, width = eigvecs.shape
    sweeps, blocks, band = reflectors.shape
    padded = jnp.concatenate([eigvecs, jnp.zeros((sweeps, width), eigvecs.dtype)], axis=0)

    def one_sweep(turn, current):
        sweep_at = (sweeps - 1 - turn).astype(jnp.int32)
        segment = lax.dynamic_slice_in_dim(current, sweep_at, total, 0).reshape(blocks, band, width)
        vectors = lax.dynamic_index_in_dim(reflectors, sweep_at, 0, keepdims=False)
        segment = apply_blocks(vectors, segment)
        return lax.dynamic_update_slice_in_dim(current, segment.reshape(total, width), sweep_at, 0)

    padded = lax.fori_loop(0, sweeps, one_sweep, padded)
    return padded[:total]
```

```python
import functools
import jax, jax.numpy as jnp
from jax import lax
from jax.experimental import pallas as pl
from jax.experimental.pallas import tpu as pltpu

S, B = 16, 64

def bcast(tile, i, ng):
    lo = jnp.broadcast_to(tile[:, i:i+1], (16, 128))
    if ng == 2:
        return lo
    hi = jnp.broadcast_to(tile[:, 64+i:65+i], (16, 128))
    return jnp.concatenate([lo, hi], 0)

def taus(tile, ng):
    sq = tile * tile
    lo = 2.0 / jnp.sum(sq[:, :64], axis=1, keepdims=True)
    lo = jnp.broadcast_to(lo, (16, 128))
    if ng == 2:
        return lo
    hi = 2.0 / jnp.sum(sq[:, 64:], axis=1, keepdims=True)
    return jnp.concatenate([lo, jnp.broadcast_to(hi, (16, 128))], 0)

def sweep_body(j, g_ref, t_ref, ng, nacc=4):
    tile = g_ref[j]
    acc = [None] * nacc
    for i in range(B):
        p = bcast(tile, i, ng) * t_ref[j + i] if i else t_ref[j]
        a = i % nacc
        acc[a] = p if acc[a] is None else acc[a] + p
    while len(acc) > 1:
        acc = [acc[a] + acc[a+1] for a in range(0, len(acc), 2)]
    w = acc[0] * taus(tile, ng)
    for i in range(B):
        t_ref[j + i] = t_ref[j + i] - (bcast(tile, i, ng) * w if i else w)

def k_all(x_ref, g_ref, halo_ref, out_ref, ret_ref, t_ref):
    ng = 4
    def load(b, c):
        t_ref[b] = x_ref[pl.ds(b, 32, stride=64), :]
        return c
    lax.fori_loop(0, 64, load, 0, unroll=8)
    last = lax.broadcasted_iota(jnp.int32, (32, 128), 0) == 31
    for i in range(15):
        r = pltpu.roll(t_ref[i], 31, 0)
        t_ref[64 + i] = jnp.where(last, jnp.broadcast_to(halo_ref[i:i+1, :], (32, 128)), r)
    def sweep(n, c):
        j = S - 1 - n
        sweep_body(j, g_ref, t_ref, ng)
        @pl.when(j > 0)
        def _():
            e = t_ref[j + 63]
            t_ref[j - 1] = pltpu.roll(e, 1, 0)
            ret_ref[pl.ds(j - 1, 1), :] = e[31:32, :]
        return c
    lax.fori_loop(0, S, sweep, 0)
    def store(b, c):
        out_ref[pl.ds(b, 16, stride=64), :] = t_ref[b, 16:, :]
        return c
    lax.fori_loop(0, 64, store, 0, unroll=8)

def call_all(x, g, halo):
    return pl.pallas_call(
        k_all,
        out_shape=(jax.ShapeDtypeStruct((2048, 128), jnp.float32), jax.ShapeDtypeStruct((16, 128), jnp.float32)),
        grid=(1,),
        in_specs=[pl.BlockSpec((2048, 128), lambda i: (0, 0)), pl.BlockSpec((16, 16, 128), lambda i: (0, 0, 0)), pl.BlockSpec((16, 128), lambda i: (0, 0))],
        out_specs=(pl.BlockSpec((1024, 128), lambda i: (1, 0)), pl.BlockSpec((16, 128), lambda i: (0, 0))),
        scratch_shapes=[pltpu.VMEM((80, 32, 128), jnp.float32)],
        name="upper",
    )(x, g, halo)

def k_low(x_ref, g_ref, ret_ref, prev_ref, out_ref, t_ref):
    ng = 2
    def load(b, c):
        t_ref[b] = x_ref[pl.ds(b, 16, stride=64), :]
        return c
    lax.fori_loop(0, 64, load, 0, unroll=8)
    last = lax.broadcasted_iota(jnp.int32, (16, 128), 0) == 15
    first = lax.broadcasted_iota(jnp.int32, (16, 128), 0) == 0
    for i in range(15):
        r = pltpu.roll(t_ref[i], 15, 0)
        t_ref[64 + i] = jnp.where(last, jnp.broadcast_to(x_ref[1024 + i:1025 + i, :], (16, 128)), r)
    def sweep(n, c):
        j = S - 1 - n
        sweep_body(j, g_ref, t_ref, ng)
        @pl.when(j > 0)
        def _():
            t_ref[j - 1] = jnp.where(first, jnp.broadcast_to(ret_ref[pl.ds(j - 1, 1), :], (16, 128)), pltpu.roll(t_ref[j + 63], 1, 0))
        return c
    lax.fori_loop(0, S, sweep, 0)
    def store(b, c):
        out_ref[pl.ds(b, 16, stride=64), :] = t_ref[b]
        return c
    lax.fori_loop(0, 64, store, 0, unroll=8)

def call_low(x, g, ret, prev):
    return pl.pallas_call(
        k_low,
        out_shape=jax.ShapeDtypeStruct((2048, 128), jnp.float32),
        grid=(1,),
        in_specs=[pl.BlockSpec((1040, 128), lambda i: (0, 0)), pl.BlockSpec((16, 16, 128), lambda i: (0, 0, 0)), pl.BlockSpec((16, 128), lambda i: (0, 0)), pl.BlockSpec(memory_space=pl.ANY)],
        out_specs=pl.BlockSpec((1024, 128), lambda i: (0, 0)),
        scratch_shapes=[pltpu.VMEM((80, 16, 128), jnp.float32)],
        input_output_aliases={3: 0},
        name="lower",
    )(x, g, ret, prev)

from jax.sharding import PartitionSpec as P


def neighbour(value, step):
    owners = lax.axis_size("row")
    return lax.ppermute(value, "row", [(i, (i + step) % owners) for i in range(owners)])


def local(eigvecs, reflectors):
    half = reflectors.shape[1] // 2
    packed = jnp.concatenate([reflectors[:, :half], reflectors[:, half:]], axis=2)
    copies = jnp.broadcast_to(packed, (lax.axis_size("col"),) + packed.shape[1:])
    halo = neighbour(eigvecs[:16], -1)
    vectors = lax.all_to_all(copies, "col", 0, 0, tiled=True)
    upper, leaving = call_all(eigvecs, vectors, halo)
    entering = neighbour(leaving, 1)
    return call_low(eigvecs, vectors, entering, upper)


def solution(mesh):
    return jax.shard_map(
        local,
        mesh=mesh,
        in_specs=(P("row", "col"), P("col", "row", None)),
        out_specs=P("row", "col"),
        check_vma=False,
    )
```

```python
import jax
import jax.numpy as jnp
from jax import lax
from jax.experimental import pallas as pl
from jax.experimental.pallas import tpu as pltpu
from jax.sharding import PartitionSpec as P

SWEEPS, BAND, HALF, LANES = 16, 64, 16, 128
TILE = (16, 128)


def lane_ids(shape=TILE):
    return lax.broadcasted_iota(jnp.int32, shape, len(shape) - 1)


def swap_slots(tiles):
    slot = lane_ids() // HALF
    tiles = list(tiles)
    for s in (4, 2, 1):
        low = slot % (2 * s) < s
        for p in range(8):
            if p & s:
                continue
            a, b = tiles[p], tiles[p | s]
            tiles[p] = jnp.where(low, a, pltpu.roll(b, HALF * s, 1))
            tiles[p | s] = jnp.where(low, pltpu.roll(a, LANES - HALF * s, 1), b)
    return tiles


def pack_kernel(reflectors_ref, copies_ref, turned_ref):
    vectors = reflectors_ref[0]
    first = lax.broadcasted_iota(jnp.int32, vectors.shape, 1) == 0
    vectors = jnp.where(first, jnp.ones_like(vectors), vectors)
    vectors = vectors * jnp.sqrt(2.0 / jnp.sum(vectors * vectors, axis=1, keepdims=True))
    padded = jnp.concatenate([vectors, jnp.zeros_like(vectors)], axis=1)
    padded = jnp.concatenate([padded] + [jnp.zeros_like(padded)] * 3, axis=0)
    turned_ref[...] = padded.T
    slot = lane_ids((8, LANES)) // HALF
    for half in range(2):
        packed = jnp.zeros((8, LANES), jnp.float32)
        for b in range(8):
            entries = turned_ref[pl.ds(b, 8, stride=8), :]
            entries = pltpu.roll(entries, (HALF * (b - half)) % LANES, 1)
            packed = jnp.where(slot == b, entries, packed)
        for sweep in range(SWEEPS):
            copies_ref[sweep, 8 * half : 8 * (half + 1), :] = packed


def pack(reflectors):
    return pl.pallas_call(
        pack_kernel,
        out_shape=jax.ShapeDtypeStruct((SWEEPS, 16, LANES), jnp.float32),
        scratch_shapes=[pltpu.VMEM((LANES, LANES), jnp.float32)],
        name="pack",
    )(reflectors)


def turn_kernel(rows_ref, tiles_ref, gathered_ref):
    for half in range(2):
        for o in range(8):
            for b in range(8):
                gathered_ref[half, o, HALF * b : HALF * (b + 1), :] = rows_ref[
                    pl.ds(half * HALF * BAND + 8 * o + b, HALF, stride=BAND), :
                ]
            turned = gathered_ref[half, o].T
            tiles = swap_slots([turned[HALF * g : HALF * (g + 1)] for g in range(8)])
            for b in range(8):
                tiles_ref[half, 8 * o + b] = tiles[b]


def turn(rows):
    return pl.pallas_call(
        turn_kernel,
        out_shape=jax.ShapeDtypeStruct((2, BAND) + TILE, jnp.float32),
        scratch_shapes=[pltpu.VMEM((2, 8, LANES, LANES), jnp.float32)],
        name="turn",
    )(rows)


def turn_back(state_ref, gathered_ref, out_ref):
    for o in range(8):
        tiles = swap_slots([state_ref[8 * o + b] for b in range(8)])
        gathered_ref[o] = jnp.concatenate(tiles, axis=0).T
        for b in range(8):
            out_ref[pl.ds(8 * o + b, HALF, stride=BAND), :] = gathered_ref[o, HALF * b : HALF * (b + 1), :]


def spread(vectors_ref, half, spread_ref):
    slot = lane_ids((8, LANES)) // HALF
    for sweep in range(SWEEPS):
        packed = vectors_ref[sweep, 8 * half : 8 * (half + 1), :]
        turns = [packed] + [pltpu.roll(packed, HALF * s, 1) for s in range(1, 8)]
        for b in range(8):
            tile = turns[(-b) % 8]
            for g in range(1, 8):
                tile = jnp.where(slot == g, turns[(g - b) % 8], tile)
            spread_ref[sweep, 8 * b : 8 * (b + 1), :] = tile


def entry(spread_ref, sweep, i):
    at = 8 * (i % 8) + i // 8
    return jnp.broadcast_to(spread_ref[sweep, at : at + 1, :], TILE)


def add_up(terms):
    while len(terms) > 1:
        terms = [sum(terms[t + 1 : t + 2], terms[t]) for t in range(0, len(terms), 2)]
    return terms[0]


def sweep_all(state_ref, spread_ref, entering):
    head = lane_ids() % HALF == 0
    sums = [None] * 4

    def add(sums, i, term):
        sums[i % 4] = term if sums[i % 4] is None else sums[i % 4] + term

    for i in range(BAND):
        add(sums, i, entry(spread_ref, SWEEPS - 1, i) * state_ref[SWEEPS - 1 + i])
    total = add_up(sums)
    for sweep in range(SWEEPS - 1, 0, -1):
        last = state_ref[sweep + BAND - 1] - entry(spread_ref, sweep, BAND - 1) * total
        state_ref[sweep + BAND - 1] = last
        first = pltpu.roll(last, 1, 1)
        if entering is not None:
            first = jnp.where(head, entering[sweep - 1], first)
        state_ref[sweep - 1] = first
        sums = [None] * 4
        for i in range(BAND - 1):
            row = state_ref[sweep + i] - entry(spread_ref, sweep, i) * total
            state_ref[sweep + i] = row
            add(sums, i, entry(spread_ref, sweep - 1, i + 1) * row)
        total = add_up(sums) + entry(spread_ref, sweep - 1, 0) * first
    for i in range(BAND):
        state_ref[i] = state_ref[i] - entry(spread_ref, 0, i) * total


def start(tiles_ref, half, after, state_ref):
    tail = lane_ids() % HALF == HALF - 1
    state_ref[:BAND] = tiles_ref[half]
    for i in range(SWEEPS - 1):
        state_ref[BAND + i] = jnp.where(tail, after[i], pltpu.roll(tiles_ref[half, i], LANES - 1, 1))


def halo_tiles(halo_ref, gathered_ref):
    gathered_ref[0, :HALF, :] = halo_ref[...]
    turned = gathered_ref[0].T
    slot = lane_ids() // HALF
    tile = turned[:HALF]
    for g in range(1, 8):
        tile = jnp.where(slot == g, pltpu.roll(turned[HALF * g : HALF * (g + 1)], HALF * g, 1), tile)
    return [pltpu.roll(tile, HALF - 1 - i, 1) for i in range(SWEEPS - 1)]


def leave_kernel(tiles_ref, vectors_ref, halo_ref, leaving_ref, state_ref, spread_ref, gathered_ref):
    gathered_ref[0] = jnp.zeros((LANES, LANES), jnp.float32)
    start(tiles_ref, 1, halo_tiles(halo_ref, gathered_ref), state_ref)
    spread(vectors_ref, 1, spread_ref)
    sweep_all(state_ref, spread_ref, None)
    place = lane_ids() % HALF
    leaving = jnp.zeros(TILE, jnp.float32)
    for i in range(SWEEPS - 1):
        leaving = jnp.where(place == i, pltpu.roll(state_ref[BAND + i], (i - HALF + 1) % LANES, 1), leaving)
    leaving_ref[...] = leaving


STATE = [
    pltpu.VMEM((BAND + SWEEPS,) + TILE, jnp.float32),
    pltpu.VMEM((SWEEPS, BAND, LANES), jnp.float32),
    pltpu.VMEM((8, LANES, LANES), jnp.float32),
]


def leave(tiles, vectors, halo):
    return pl.pallas_call(
        leave_kernel,
        out_shape=jax.ShapeDtypeStruct(TILE, jnp.float32),
        scratch_shapes=STATE,
        name="leave",
    )(tiles, vectors, halo)


def upper_kernel(tiles_ref, vectors_ref, halo_ref, out_ref, lower_ref, state_ref, spread_ref, gathered_ref):
    start(tiles_ref, 0, [pltpu.roll(tiles_ref[1, i], HALF - 1, 1) for i in range(SWEEPS - 1)], lower_ref)
    spread(vectors_ref, 0, spread_ref)
    sweep_all(lower_ref, spread_ref, None)
    gathered_ref[0] = jnp.zeros((LANES, LANES), jnp.float32)
    start(tiles_ref, 1, halo_tiles(halo_ref, gathered_ref), state_ref)
    spread(vectors_ref, 1, spread_ref)
    sweep_all(
        state_ref,
        spread_ref,
        [pltpu.roll(lower_ref[BAND + i], LANES - HALF + 1, 1) for i in range(SWEEPS - 1)],
    )
    turn_back(state_ref, gathered_ref, out_ref)


def upper(tiles, vectors, halo):
    return pl.pallas_call(
        upper_kernel,
        out_shape=jax.ShapeDtypeStruct((2 * HALF * BAND, LANES), jnp.float32),
        grid=(1,),
        in_specs=[pl.BlockSpec(tiles.shape, lambda i: (0, 0, 0, 0)), pl.BlockSpec(vectors.shape, lambda i: (0, 0, 0)), pl.BlockSpec(halo.shape, lambda i: (0, 0))],
        out_specs=pl.BlockSpec((HALF * BAND, LANES), lambda i: (1, 0)),
        scratch_shapes=[STATE[0]] + STATE,
        name="upper",
    )(tiles, vectors, halo)


def lower_kernel(tiles_ref, vectors_ref, entering_ref, upper_ref, out_ref, state_ref, spread_ref, gathered_ref):
    start(tiles_ref, 0, [pltpu.roll(tiles_ref[1, i], HALF - 1, 1) for i in range(SWEEPS - 1)], state_ref)
    spread(vectors_ref, 0, spread_ref)
    entering = entering_ref[...]
    sweep_all(state_ref, spread_ref, [pltpu.roll(entering, (-i) % LANES, 1) for i in range(SWEEPS - 1)])
    turn_back(state_ref, gathered_ref, out_ref)


def lower(tiles, vectors, entering, upper_rows):
    return pl.pallas_call(
        lower_kernel,
        out_shape=jax.ShapeDtypeStruct((2 * HALF * BAND, LANES), jnp.float32),
        grid=(1,),
        in_specs=[pl.BlockSpec(tiles.shape, lambda i: (0, 0, 0, 0)), pl.BlockSpec(vectors.shape, lambda i: (0, 0, 0)), pl.BlockSpec(entering.shape, lambda i: (0, 0)), pl.BlockSpec(memory_space=pl.ANY)],
        out_specs=pl.BlockSpec((HALF * BAND, LANES), lambda i: (0, 0)),
        scratch_shapes=STATE,
        input_output_aliases={3: 0},
        name="lower",
    )(tiles, vectors, entering, upper_rows)


def neighbour(value, step):
    owners = lax.axis_size("row")
    return lax.ppermute(value, "row", [(i, (i + step) % owners) for i in range(owners)])


def local(eigvecs, reflectors):
    copies = pack(reflectors)
    halo = neighbour(eigvecs[:SWEEPS], -1)
    vectors = lax.all_to_all(copies, "col", 0, 0, tiled=True)
    tiles = turn(eigvecs)
    leaving = leave(tiles, vectors, halo)
    entering = neighbour(leaving, 1)
    upper_rows = upper(tiles, vectors, halo)
    return lower(tiles, vectors, entering, upper_rows)


def solution(mesh):
    return jax.shard_map(
        local,
        mesh=mesh,
        in_specs=(P("row", "col"), P("col", "row", None)),
        out_specs=P("row", "col"),
        check_vma=False,
    )
```

```python
import jax
import jax.numpy as jnp
from jax import lax
from jax.experimental import pallas as pl
from jax.experimental.pallas import tpu as pltpu
from jax.sharding import PartitionSpec as P

SWEEPS, BAND, HALF, LANES = 16, 64, 16, 128
TILE = (16, 128)


def lane_ids(shape=TILE):
    return lax.broadcasted_iota(jnp.int32, shape, len(shape) - 1)


def swap_slots(tiles):
    slot = lane_ids() // HALF
    tiles = list(tiles)
    for s in (4, 2, 1):
        low = slot % (2 * s) < s
        for p in range(8):
            if p & s:
                continue
            a, b = tiles[p], tiles[p | s]
            tiles[p] = jnp.where(low, a, pltpu.roll(b, HALF * s, 1))
            tiles[p | s] = jnp.where(low, pltpu.roll(a, LANES - HALF * s, 1), b)
    return tiles


def pack_kernel(reflectors_ref, copies_ref, turned_ref):
    vectors = reflectors_ref[0]
    first = lax.broadcasted_iota(jnp.int32, vectors.shape, 1) == 0
    vectors = jnp.where(first, jnp.ones_like(vectors), vectors)
    vectors = vectors * jnp.sqrt(2.0 / jnp.sum(vectors * vectors, axis=1, keepdims=True))
    padded = jnp.concatenate([vectors, jnp.zeros_like(vectors)], axis=1)
    padded = jnp.concatenate([padded] + [jnp.zeros_like(padded)] * 3, axis=0)
    turned_ref[...] = padded.T
    slot = lane_ids((8, LANES)) // HALF
    for half in range(2):
        packed = jnp.zeros((8, LANES), jnp.float32)
        for b in range(8):
            entries = turned_ref[pl.ds(b, 8, stride=8), :]
            entries = pltpu.roll(entries, (HALF * (b - half)) % LANES, 1)
            packed = jnp.where(slot == b, entries, packed)
        for sweep in range(SWEEPS):
            copies_ref[sweep, 8 * half : 8 * (half + 1), :] = packed


def pack(reflectors):
    return pl.pallas_call(
        pack_kernel,
        out_shape=jax.ShapeDtypeStruct((SWEEPS, 16, LANES), jnp.float32),
        scratch_shapes=[pltpu.VMEM((LANES, LANES), jnp.float32)],
        name="pack",
        compiler_params=pltpu.CompilerParams(vmem_limit_bytes=8 * 2**20),
    )(reflectors)


def turn_kernel(rows_ref, tiles_ref, gathered_ref):
    for half in range(2):
        for o in range(8):
            for b in range(8):
                gathered_ref[half, o, HALF * b : HALF * (b + 1), :] = rows_ref[
                    pl.ds(half * HALF * BAND + 8 * o + b, HALF, stride=BAND), :
                ]
            turned = gathered_ref[half, o].T
            tiles = swap_slots([turned[HALF * g : HALF * (g + 1)] for g in range(8)])
            for b in range(8):
                tiles_ref[half, 8 * o + b] = tiles[b]


def turn(rows):
    return pl.pallas_call(
        turn_kernel,
        out_shape=jax.ShapeDtypeStruct((2, BAND) + TILE, jnp.float32),
        scratch_shapes=[pltpu.VMEM((2, 8, LANES, LANES), jnp.float32)],
        name="turn",
        compiler_params=pltpu.CompilerParams(vmem_limit_bytes=8 * 2**20),
    )(rows)


def turn_back(state_ref, gathered_ref, out_ref):
    for o in range(8):
        tiles = swap_slots([state_ref[8 * o + b] for b in range(8)])
        gathered_ref[o] = jnp.concatenate(tiles, axis=0).T
        for b in range(8):
            out_ref[pl.ds(8 * o + b, HALF, stride=BAND), :] = gathered_ref[o, HALF * b : HALF * (b + 1), :]


def spread(vectors_ref, half, spread_ref):
    slot = lane_ids((8, LANES)) // HALF
    for sweep in range(SWEEPS):
        packed = vectors_ref[sweep, 8 * half : 8 * (half + 1), :]
        turns = [packed] + [pltpu.roll(packed, HALF * s, 1) for s in range(1, 8)]
        for b in range(8):
            tile = turns[(-b) % 8]
            for g in range(1, 8):
                tile = jnp.where(slot == g, turns[(g - b) % 8], tile)
            spread_ref[sweep, 8 * b : 8 * (b + 1), :] = tile


def entry(spread_ref, sweep, i):
    at = 8 * (i % 8) + i // 8
    return jnp.broadcast_to(spread_ref[sweep, at : at + 1, :], TILE)


def add_up(terms):
    while len(terms) > 1:
        terms = [sum(terms[t + 1 : t + 2], terms[t]) for t in range(0, len(terms), 2)]
    return terms[0]


def sweep_all(state_ref, spread_ref, entering):
    head = lane_ids() % HALF == 0
    sums = [None] * 4

    def add(sums, i, term):
        sums[i % 4] = term if sums[i % 4] is None else sums[i % 4] + term

    for i in range(BAND):
        add(sums, i, entry(spread_ref, SWEEPS - 1, i) * state_ref[SWEEPS - 1 + i])
    total = add_up(sums)
    for sweep in range(SWEEPS - 1, 0, -1):
        last = state_ref[sweep + BAND - 1] - entry(spread_ref, sweep, BAND - 1) * total
        state_ref[sweep + BAND - 1] = last
        first = pltpu.roll(last, 1, 1)
        if entering is not None:
            first = jnp.where(head, entering[sweep - 1], first)
        state_ref[sweep - 1] = first
        sums = [None] * 4
        for i in range(BAND - 1):
            row = state_ref[sweep + i] - entry(spread_ref, sweep, i) * total
            state_ref[sweep + i] = row
            add(sums, i, entry(spread_ref, sweep - 1, i + 1) * row)
        total = add_up(sums) + entry(spread_ref, sweep - 1, 0) * first
    for i in range(BAND):
        state_ref[i] = state_ref[i] - entry(spread_ref, 0, i) * total


def start(tiles_ref, half, after, state_ref):
    tail = lane_ids() % HALF == HALF - 1
    state_ref[:BAND] = tiles_ref[half]
    for i in range(SWEEPS - 1):
        state_ref[BAND + i] = jnp.where(tail, after[i], pltpu.roll(tiles_ref[half, i], LANES - 1, 1))


def halo_tiles(halo_ref, gathered_ref):
    gathered_ref[0, :HALF, :] = halo_ref[...]
    turned = gathered_ref[0].T
    slot = lane_ids() // HALF
    tile = turned[:HALF]
    for g in range(1, 8):
        tile = jnp.where(slot == g, pltpu.roll(turned[HALF * g : HALF * (g + 1)], HALF * g, 1), tile)
    return [pltpu.roll(tile, HALF - 1 - i, 1) for i in range(SWEEPS - 1)]


def leave_kernel(tiles_ref, vectors_ref, halo_ref, leaving_ref, state_ref, spread_ref, gathered_ref):
    gathered_ref[0] = jnp.zeros((LANES, LANES), jnp.float32)
    start(tiles_ref, 1, halo_tiles(halo_ref, gathered_ref), state_ref)
    spread(vectors_ref, 1, spread_ref)
    sweep_all(state_ref, spread_ref, None)
    place = lane_ids() % HALF
    leaving = jnp.zeros(TILE, jnp.float32)
    for i in range(SWEEPS - 1):
        leaving = jnp.where(place == i, pltpu.roll(state_ref[BAND + i], (i - HALF + 1) % LANES, 1), leaving)
    leaving_ref[...] = leaving


STATE = [
    pltpu.VMEM((BAND + SWEEPS,) + TILE, jnp.float32),
    pltpu.VMEM((SWEEPS, BAND, LANES), jnp.float32),
    pltpu.VMEM((8, LANES, LANES), jnp.float32),
]


def leave(tiles, vectors, halo):
    return pl.pallas_call(
        leave_kernel,
        out_shape=jax.ShapeDtypeStruct(TILE, jnp.float32),
        scratch_shapes=STATE,
        name="leave",
        compiler_params=pltpu.CompilerParams(vmem_limit_bytes=8 * 2**20),
    )(tiles, vectors, halo)


def upper_kernel(tiles_ref, vectors_ref, halo_ref, out_ref, lower_ref, state_ref, spread_ref, gathered_ref):
    start(tiles_ref, 0, [pltpu.roll(tiles_ref[1, i], HALF - 1, 1) for i in range(SWEEPS - 1)], lower_ref)
    spread(vectors_ref, 0, spread_ref)
    sweep_all(lower_ref, spread_ref, None)
    gathered_ref[0] = jnp.zeros((LANES, LANES), jnp.float32)
    start(tiles_ref, 1, halo_tiles(halo_ref, gathered_ref), state_ref)
    spread(vectors_ref, 1, spread_ref)
    sweep_all(
        state_ref,
        spread_ref,
        [pltpu.roll(lower_ref[BAND + i], LANES - HALF + 1, 1) for i in range(SWEEPS - 1)],
    )
    turn_back(state_ref, gathered_ref, out_ref)


def upper(tiles, vectors, halo):
    return pl.pallas_call(
        upper_kernel,
        out_shape=jax.ShapeDtypeStruct((2 * HALF * BAND, LANES), jnp.float32),
        grid=(1,),
        in_specs=[pl.BlockSpec(tiles.shape, lambda i: (0, 0, 0, 0)), pl.BlockSpec(vectors.shape, lambda i: (0, 0, 0)), pl.BlockSpec(halo.shape, lambda i: (0, 0))],
        out_specs=pl.BlockSpec((HALF * BAND, LANES), lambda i: (1, 0)),
        scratch_shapes=[STATE[0]] + STATE,
        name="upper",
        compiler_params=pltpu.CompilerParams(vmem_limit_bytes=8 * 2**20),
    )(tiles, vectors, halo)


def lower_kernel(tiles_ref, vectors_ref, entering_ref, upper_ref, out_ref, state_ref, spread_ref, gathered_ref):
    start(tiles_ref, 0, [pltpu.roll(tiles_ref[1, i], HALF - 1, 1) for i in range(SWEEPS - 1)], state_ref)
    spread(vectors_ref, 0, spread_ref)
    entering = entering_ref[...]
    sweep_all(state_ref, spread_ref, [pltpu.roll(entering, (-i) % LANES, 1) for i in range(SWEEPS - 1)])
    turn_back(state_ref, gathered_ref, out_ref)


def lower(tiles, vectors, entering, upper_rows):
    return pl.pallas_call(
        lower_kernel,
        out_shape=jax.ShapeDtypeStruct((2 * HALF * BAND, LANES), jnp.float32),
        grid=(1,),
        in_specs=[pl.BlockSpec(tiles.shape, lambda i: (0, 0, 0, 0)), pl.BlockSpec(vectors.shape, lambda i: (0, 0, 0)), pl.BlockSpec(entering.shape, lambda i: (0, 0)), pl.BlockSpec(memory_space=pl.ANY)],
        out_specs=pl.BlockSpec((HALF * BAND, LANES), lambda i: (0, 0)),
        scratch_shapes=STATE,
        input_output_aliases={3: 0},
        name="lower",
        compiler_params=pltpu.CompilerParams(vmem_limit_bytes=8 * 2**20),
    )(tiles, vectors, entering, upper_rows)


def neighbour(value, step):
    owners = lax.axis_size("row")
    return lax.ppermute(value, "row", [(i, (i + step) % owners) for i in range(owners)])


def local(eigvecs, reflectors):
    copies = pack(reflectors)
    halo = neighbour(eigvecs[:SWEEPS], -1)
    vectors = lax.all_to_all(copies, "col", 0, 0, tiled=True)
    tiles = turn(eigvecs)
    leaving = leave(tiles, vectors, halo)
    entering = neighbour(leaving, 1)
    upper_rows = upper(tiles, vectors, halo)
    return lower(tiles, vectors, entering, upper_rows)


def solution(mesh):
    return jax.shard_map(
        local,
        mesh=mesh,
        in_specs=(P("row", "col"), P("col", "row", None)),
        out_specs=P("row", "col"),
        check_vma=False,
    )
```

```python
import jax
import jax.numpy as jnp
from jax import lax
from jax.experimental import pallas as pl
from jax.experimental.pallas import tpu as pltpu
from jax.sharding import PartitionSpec as P

SWEEPS, BAND, HALF, LANES = 16, 64, 16, 128
TILE = (16, 128)
EARLY = 6


def is_early():
    row, column = lax.axis_index("row"), lax.axis_index("col")
    return jnp.logical_and(column < EARLY, row + column > 0)


PARAMS = pltpu.CompilerParams(vmem_limit_bytes=8 * 2**20)


def lane_ids(shape=TILE):
    return lax.broadcasted_iota(jnp.int32, shape, len(shape) - 1)


def swap_slots(tiles):
    slot = lane_ids() // HALF
    skewed = [pltpu.roll(tiles[p], HALF * p, 1) if p else tiles[p] for p in range(8)]
    skewed = [skewed[-t % 8] for t in range(8)]
    for s in (1, 2, 4):
        moved = slot & s != 0
        skewed = [jnp.where(moved, skewed[(t - s) % 8], skewed[t]) for t in range(8)]
    return [pltpu.roll(skewed[q], LANES - HALF * q, 1) if q else skewed[q] for q in range(8)]


def pack_kernel(reflectors_ref, copies_ref, turned_ref):
    vectors = reflectors_ref[0]
    first = lax.broadcasted_iota(jnp.int32, vectors.shape, 1) == 0
    vectors = jnp.where(first, jnp.ones_like(vectors), vectors)
    vectors = vectors * jnp.sqrt(2.0 / jnp.sum(vectors * vectors, axis=1, keepdims=True))
    padded = jnp.concatenate([vectors, jnp.zeros_like(vectors)], axis=1)
    padded = jnp.concatenate([padded] + [jnp.zeros_like(padded)] * 3, axis=0)
    turned_ref[...] = padded.T
    slot = lane_ids((8, LANES)) // HALF
    for half in range(2):
        packed = jnp.zeros((8, LANES), jnp.float32)
        for b in range(8):
            entries = turned_ref[pl.ds(b, 8, stride=8), :]
            entries = pltpu.roll(entries, (HALF * (b - half)) % LANES, 1)
            packed = jnp.where(slot == b, entries, packed)
        for sweep in range(SWEEPS):
            copies_ref[sweep, 8 * half : 8 * (half + 1), :] = packed


def pack(reflectors):
    return pl.pallas_call(
        pack_kernel,
        out_shape=jax.ShapeDtypeStruct((SWEEPS, 16, LANES), jnp.float32),
        scratch_shapes=[pltpu.VMEM((LANES, LANES), jnp.float32)],
        name="pack",
        compiler_params=PARAMS,
    )(reflectors)


def turn_rows(rows_ref, landed_ref, gathered_ref, tiles_ref, arrived):
    pieces = [pl.ds(half * HALF * BAND, HALF * BAND) for half in range(2)]
    copies = [
        pltpu.make_async_copy(rows_ref.at[piece], landed_ref.at[piece], arrived.at[half])
        for half, piece in enumerate(pieces)
    ]
    for copy in copies:
        copy.start()
    for half in range(2):
        copies[half].wait()
        for o in range(8):
            for b in range(8):
                gathered_ref[half, o, HALF * b : HALF * (b + 1), :] = landed_ref[
                    pl.ds(half * HALF * BAND + 8 * o + b, HALF, stride=BAND), :
                ]
            turned = gathered_ref[half, o].T
            tiles = swap_slots([turned[HALF * g : HALF * (g + 1)] for g in range(8)])
            for b in range(8):
                tiles_ref[half, 8 * o + b] = tiles[b]


def turn_early_kernel(rows_ref, tiles_ref, landed_ref, gathered_ref, arrived, turned_ref, left):
    @pl.when(is_early())
    def _():
        turn_rows(rows_ref, landed_ref, gathered_ref, turned_ref, arrived)
        copy = pltpu.make_async_copy(turned_ref, tiles_ref, left)
        copy.start()
        copy.wait()


def turn_late_kernel(rows_ref, early_ref, tiles_ref, *scratch):
    arrived = scratch[2]
    @pl.when(jnp.logical_not(is_early()))
    def _():
        turn_rows(rows_ref, scratch[0], scratch[1], tiles_ref, scratch[2])

    @pl.when(is_early())
    def _():
        copies = [pltpu.make_async_copy(early_ref.at[half], tiles_ref.at[half], arrived.at[half]) for half in range(2)]
        for copy in copies:
            copy.start()
        for copy in copies:
            copy.wait()


TURN = dict(
    out_shape=jax.ShapeDtypeStruct((2, BAND) + TILE, jnp.float32),
    scratch_shapes=[
        pltpu.VMEM((2 * HALF * BAND, LANES), jnp.float32),
        pltpu.VMEM((2, 8, LANES, LANES), jnp.float32),
        pltpu.SemaphoreType.DMA((2,)),
    ],
    compiler_params=PARAMS,
)


def turn_early(rows):
    return pl.pallas_call(
        turn_early_kernel,
        out_shape=TURN["out_shape"],
        in_specs=[pl.BlockSpec(memory_space=pl.ANY)],
        out_specs=pl.BlockSpec(memory_space=pl.ANY),
        scratch_shapes=TURN["scratch_shapes"] + [pltpu.VMEM((2, BAND) + TILE, jnp.float32), pltpu.SemaphoreType.DMA],
        name="turn_early",
        compiler_params=pltpu.CompilerParams(vmem_limit_bytes=56 * 2**20),
    )(rows)


def turn_late(rows, early):
    return pl.pallas_call(
        turn_late_kernel,
        in_specs=[pl.BlockSpec(memory_space=pl.ANY)] * 2,
        name="turn_late",
        **TURN,
    )(rows, early)


def turn_back(turned, rows_ref, out_ref, half, o, sent):
    rows = turned.T
    for b in range(8):
        rows_ref[o, pl.ds(b, HALF, stride=8), :] = rows[HALF * b : HALF * (b + 1)]
    copy = pltpu.make_async_copy(
        rows_ref.at[o].reshape(HALF, 8, LANES),
        out_ref.at[pl.ds(HALF * half, HALF), pl.ds(8 * o, 8)],
        sent.at[o],
    )
    copy.start()
    return copy


def rows_after(state_ref):
    place = lane_ids() % HALF
    tile = jnp.zeros(TILE, jnp.float32)
    for i in range(SWEEPS - 1):
        tile = jnp.where(place == i, pltpu.roll(state_ref[BAND + i], (i - HALF + 1) % LANES, 1), tile)
    return tile


def spread(vectors_ref, half, sweep):
    slot = lane_ids((8, LANES)) // HALF
    packed = vectors_ref[sweep, 8 * half : 8 * (half + 1), :]
    turns = [packed] + [pltpu.roll(packed, HALF * s, 1) for s in range(1, 8)]
    tiles = []
    for b in range(8):
        tile = turns[(-b) % 8]
        for g in range(1, 8):
            tile = jnp.where(slot == g, turns[(g - b) % 8], tile)
        tiles.append(tile)
    return tiles


def add_up(terms):
    while len(terms) > 1:
        terms = [sum(terms[t + 1 : t + 2], terms[t]) for t in range(0, len(terms), 2)]
    return terms[0]


def sweep_all(state_ref, spread_ref, prepare, entering, beside):
    tile = state_ref.shape[1:]
    head = lane_ids(tile) % HALF == 0
    sums = [None] * 4
    beside = list(beside)
    share = -(-len(beside) // (SWEEPS - 1))

    def entry(sweep, i):
        at = 8 * (i % 8) + i // 8
        return jnp.broadcast_to(spread_ref[sweep, at : at + 1, :], tile)

    def add(sums, i, term):
        sums[i % 4] = term if sums[i % 4] is None else sums[i % 4] + term

    for sweep in range(SWEEPS - 1, -1, -1):
        prepare(sweep)
    for i in range(BAND):
        add(sums, i, entry(SWEEPS - 1, i) * state_ref[SWEEPS - 1 + i])
    total = add_up(sums)
    for sweep in range(SWEEPS - 1, 0, -1):
        last = state_ref[sweep + BAND - 1] - entry(sweep, BAND - 1) * total
        state_ref[sweep + BAND - 1] = last
        first = jnp.where(head, entering(sweep - 1), pltpu.roll(last, 1, 1))
        state_ref[sweep - 1] = first
        sums = [None] * 4
        for i in range(BAND - 1):
            row = state_ref[sweep + i] - entry(sweep, i) * total
            state_ref[sweep + i] = row
            add(sums, i, entry(sweep - 1, i + 1) * row)
        total = add_up(sums) + entry(sweep - 1, 0) * first
        for work in beside[:share]:
            work()
        beside = beside[share:]
    for i in range(BAND):
        state_ref[i] = state_ref[i] - entry(0, i) * total


def nothing(i):
    return jnp.zeros(TILE, jnp.float32)


def after_kernel(tiles_ref, halo_ref, after_ref, gathered_ref):
    last = lane_ids() % HALF == HALF - 1
    gathered_ref[...] = jnp.zeros_like(gathered_ref)
    gathered_ref[:HALF, :] = halo_ref[...]
    turned = gathered_ref[...].T
    slot = lane_ids() // HALF
    halo = turned[:HALF]
    for g in range(1, 8):
        halo = jnp.where(slot == g, pltpu.roll(turned[HALF * g : HALF * (g + 1)], HALF * g, 1), halo)
    for i in range(SWEEPS - 1):
        own = [pltpu.roll(tiles_ref[half, i], LANES - 1, 1) for half in range(2)]
        after_ref[0, i] = jnp.where(last, pltpu.roll(tiles_ref[1, i], HALF - 1, 1), own[0])
        after_ref[1, i] = jnp.where(last, pltpu.roll(halo, HALF - 1 - i, 1), own[1])


def rows_following(tiles, halo):
    return pl.pallas_call(
        after_kernel,
        out_shape=jax.ShapeDtypeStruct((2, SWEEPS - 1) + TILE, jnp.float32),
        scratch_shapes=[pltpu.VMEM((LANES, LANES), jnp.float32)],
        name="after",
        compiler_params=PARAMS,
    )(tiles, halo)


def leave_kernel(tiles_ref, vectors_ref, after_ref, leaving_ref, spread_ref, state_ref):
    state_ref[:BAND] = tiles_ref[1]
    state_ref[BAND : BAND + SWEEPS - 1] = after_ref[1]

    def prepare(sweep):
        for b, tile in enumerate(spread(vectors_ref, 1, sweep)):
            spread_ref[sweep, 8 * b : 8 * (b + 1), :] = tile

    sweep_all(state_ref, spread_ref, prepare, nothing, [])
    leaving_ref[...] = rows_after(state_ref)


STATE, SPREAD = (BAND + SWEEPS,) + TILE, (SWEEPS, BAND, LANES)
OCTS = (8, LANES, LANES)
OUT = (2 * HALF, BAND, LANES)
VMEM, ANY = pl.BlockSpec(memory_space=pltpu.VMEM), pl.BlockSpec(memory_space=pl.ANY)


def leave(tiles, vectors, after):
    return pl.pallas_call(
        leave_kernel,
        out_shape=tuple(jax.ShapeDtypeStruct(shape, jnp.float32) for shape in (TILE, SPREAD)),
        scratch_shapes=[pltpu.VMEM(STATE, jnp.float32)],
        name="leave",
        compiler_params=PARAMS,
    )(tiles, vectors, after)


def upper_kernel(
    tiles_ref, vectors_ref, after_ref, upper_spread_ref,
    out_ref, fixed_ref, response_ref,
    lower_ref, state_ref, spread_ref, rows_ref, sent,
):
    lower_ref[:, 16:, :] = jnp.zeros((BAND + SWEEPS, 8, LANES), jnp.float32)
    for i in range(BAND):
        lower_ref[i, :16, :] = tiles_ref[0, i]
    for i in range(SWEEPS - 1):
        lower_ref[BAND + i, :16, :] = after_ref[0, i]

    def prepare(sweep):
        for b, tile in enumerate(spread(vectors_ref, 0, sweep)):
            spread_ref[sweep, 8 * b : 8 * (b + 1), :] = tile

    wide = lower_ref.shape[1:]
    row, parity = lax.broadcasted_iota(jnp.int32, wide, 0), lane_ids(wide) // HALF % 2
    sweep_all(
        lower_ref,
        spread_ref,
        prepare,
        lambda i: jnp.where(jnp.logical_and(row == 16 + i % 8, parity == i // 8), 1.0, 0.0),
        [],
    )
    state_ref[:BAND] = tiles_ref[1]
    state_ref[BAND : BAND + SWEEPS - 1] = after_ref[1]
    sweep_all(
        state_ref,
        upper_spread_ref,
        lambda sweep: None,
        lambda i: pltpu.roll(lower_ref[BAND + i, :16, :], LANES - HALF + 1, 1),
        [],
    )
    copies = []
    for o in range(8):
        turned = jnp.concatenate(swap_slots([state_ref[8 * o + b] for b in range(8)]), axis=0)
        copies.append(turn_back(turned, rows_ref, out_ref, 1, o, sent))
    slot = lane_ids((8, LANES)) // HALF
    for o in range(8):
        fixed_ref[o] = jnp.concatenate(swap_slots([lower_ref[8 * o + b, :16, :] for b in range(8)]), axis=0)
        first, second = None, None
        for b in range(8):
            unit = lower_ref[8 * o + b, 16:, :]
            parts = unit, pltpu.roll(unit, HALF, 1)
            first = parts[0] if first is None else jnp.where(slot == b, parts[b % 2], first)
            second = parts[1] if second is None else jnp.where(slot == b, parts[1 - b % 2], second)
        response_ref[o, :8, :] = first
        response_ref[o, 8:, :] = second
    for copy in copies:
        copy.wait()


def upper(*operands):
    return pl.pallas_call(
        upper_kernel,
        out_shape=tuple(jax.ShapeDtypeStruct(shape, jnp.float32) for shape in (OUT, OCTS, (8,) + TILE)),
        out_specs=(ANY, VMEM, VMEM),
        scratch_shapes=[pltpu.VMEM(shape, jnp.float32) for shape in ((BAND + SWEEPS, 24, LANES), STATE, SPREAD, OCTS)]
        + [pltpu.SemaphoreType.DMA((8,))],
        name="upper",
        compiler_params=PARAMS,
    )(*operands)


def lower_kernel(fixed_ref, response_ref, entering_ref, upper_ref, out_ref, rows_ref, sent):
    tile = entering_ref[...]
    valid = lane_ids() % HALF < SWEEPS - 1
    tile = jnp.where(valid, tile, jnp.zeros_like(tile))
    entering = jnp.concatenate(
        [tile] + [pltpu.roll(tile, LANES - HALF * g, 1) for g in range(1, 8)], axis=0
    )[:, :HALF]
    copies = []
    for o in range(8):
        added = lax.dot_general(
            entering,
            response_ref[o],
            (((1,), (0,)), ((), ())),
            precision=lax.Precision.HIGHEST,
            preferred_element_type=jnp.float32,
        )
        copies.append(turn_back(fixed_ref[o] + added, rows_ref, out_ref, 0, o, sent))
    for copy in copies:
        copy.wait()


def lower(fixed, response, entering, upper_rows):
    return pl.pallas_call(
        lower_kernel,
        out_shape=jax.ShapeDtypeStruct(OUT, jnp.float32),
        in_specs=[VMEM, VMEM, VMEM, ANY],
        out_specs=ANY,
        scratch_shapes=[pltpu.VMEM(OCTS, jnp.float32), pltpu.SemaphoreType.DMA((8,))],
        input_output_aliases={3: 0},
        name="lower",
        compiler_params=PARAMS,
    )(fixed, response, entering, upper_rows)


def neighbour(value, step):
    owners = lax.axis_size("row")
    return lax.ppermute(value, "row", [(i, (i + step) % owners) for i in range(owners)])


def local(eigvecs, reflectors):
    early, copies = lax.optimization_barrier((turn_early(eigvecs), pack(reflectors)))
    vectors = lax.all_to_all(copies, "col", 0, 0, tiled=True)
    halo = neighbour(eigvecs[:SWEEPS], -1)
    return sweeps(eigvecs, early, halo, vectors)


def sweeps(eigvecs, early, halo, vectors):
    tiles = turn_late(eigvecs, early)
    after = rows_following(tiles, halo)
    leaving, upper_spread = leave(tiles, vectors, after)
    entering = neighbour(leaving, 1)
    upper_rows, fixed, response = upper(tiles, vectors, after, upper_spread)
    return lower(fixed, response, entering, upper_rows).reshape(eigvecs.shape)


def solution(mesh):
    return jax.shard_map(
        local,
        mesh=mesh,
        in_specs=(P("row", "col"), P("col", "row", None)),
        out_specs=P("row", "col"),
        check_vma=False,
    )
```

```python
import jax
import jax.numpy as jnp
from jax import lax
from jax.experimental import pallas as pl
from jax.experimental.pallas import tpu as pltpu
from jax.sharding import PartitionSpec as P

SWEEPS, BAND, HALF, LANES = 16, 64, 16, 128
TILE = (16, 128)
PARAMS = pltpu.CompilerParams(vmem_limit_bytes=8 * 2**20)


def lane_ids(shape=TILE):
    return lax.broadcasted_iota(jnp.int32, shape, len(shape) - 1)


def shear(tiles):
    slot = lane_ids(tiles[0].shape) // HALF
    for s in (1, 2, 4):
        moved = slot & s != 0
        tiles = [jnp.where(moved, tiles[(t - s) % 8], tiles[t]) for t in range(8)]
    return tiles


def swap_slots(tiles):
    tiles = shear([tiles[-t % 8] for t in range(8)])
    return shear([pltpu.roll(tiles[t], LANES - HALF * t, 1) if t else tiles[t] for t in range(8)])


def pack_kernel(reflectors_ref, copies_ref, turned_ref):
    vectors = reflectors_ref[0]
    first = lax.broadcasted_iota(jnp.int32, vectors.shape, 1) == 0
    vectors = jnp.where(first, jnp.ones_like(vectors), vectors)
    vectors = vectors * jnp.sqrt(2.0 / jnp.sum(vectors * vectors, axis=1, keepdims=True))
    padded = jnp.concatenate([vectors, jnp.zeros_like(vectors)], axis=1)
    padded = jnp.concatenate([padded] + [jnp.zeros_like(padded)] * 3, axis=0)
    turned_ref[...] = padded.T
    slot = lane_ids((8, LANES)) // HALF
    for half in range(2):
        packed = jnp.zeros((8, LANES), jnp.float32)
        for b in range(8):
            entries = turned_ref[pl.ds(b, 8, stride=8), :]
            entries = pltpu.roll(entries, (HALF * (b - half)) % LANES, 1)
            packed = jnp.where(slot == b, entries, packed)
        for sweep in range(SWEEPS):
            copies_ref[sweep, 8 * half : 8 * (half + 1), :] = packed


def pack(reflectors):
    return pl.pallas_call(
        pack_kernel,
        out_shape=jax.ShapeDtypeStruct((SWEEPS, 16, LANES), jnp.float32),
        scratch_shapes=[pltpu.VMEM((LANES, LANES), jnp.float32)],
        name="pack",
        compiler_params=PARAMS,
    )(reflectors)


def turn_kernel(rows_ref, tiles_ref, gathered_ref):
    for half in range(2):
        for o in range(8):
            for b in range(8):
                gathered_ref[half, o, HALF * b : HALF * (b + 1), :] = rows_ref[
                    pl.ds(half * HALF * BAND + 8 * o + b, HALF, stride=BAND), :
                ]
            turned = gathered_ref[half, o].T
            tiles = swap_slots([turned[HALF * g : HALF * (g + 1)] for g in range(8)])
            for b in range(8):
                tiles_ref[half, 8 * o + b] = tiles[b]


def turn(rows):
    return pl.pallas_call(
        turn_kernel,
        out_shape=jax.ShapeDtypeStruct((2, BAND) + TILE, jnp.float32),
        scratch_shapes=[pltpu.VMEM((2, 8, LANES, LANES), jnp.float32)],
        name="turn",
        compiler_params=PARAMS,
    )(rows)


def turn_back(turned, rows_ref, out_ref, half, o, sent):
    rows = turned.T
    for b in range(8):
        rows_ref[o, pl.ds(b, HALF, stride=8), :] = rows[HALF * b : HALF * (b + 1)]
    copy = pltpu.make_async_copy(
        rows_ref.at[o].reshape(HALF, 8, LANES),
        out_ref.at[pl.ds(HALF * half, HALF), pl.ds(8 * o, 8)],
        sent.at[o],
    )
    copy.start()
    return copy


def rows_after(state_ref):
    place = lane_ids() % HALF
    tile = jnp.zeros(TILE, jnp.float32)
    for i in range(SWEEPS - 1):
        tile = jnp.where(place == i, pltpu.roll(state_ref[BAND + i], (i - HALF + 1) % LANES, 1), tile)
    return tile


def spread(vectors_ref, half, sweep):
    packed = vectors_ref[sweep, 8 * half : 8 * (half + 1), :]
    return shear([pltpu.roll(packed, LANES - HALF * t, 1) if t else packed for t in range(8)])


def add_up(terms):
    while len(terms) > 1:
        terms = [sum(terms[t + 1 : t + 2], terms[t]) for t in range(0, len(terms), 2)]
    return terms[0]


def sweep_all(states, spreads, initial, entering, prepare, results):
    tiles = [state.shape[1:] for state in states]
    heads = [lane_ids(tile) % HALF == 0 for tile in tiles]
    halves = range(len(states))

    def entry(half, sweep, i):
        at = 8 * (i % 8) + i // 8
        return jnp.broadcast_to(spreads[half][sweep, at : at + 1, :], tiles[half])

    def before(half, sweep, i):
        return initial[half](i) if sweep == SWEEPS - 1 else states[half][i]

    def add(sums, i, term):
        sums[i % 2] = term if sums[i % 2] is None else sums[i % 2] + term

    if prepare:
        for sweep in range(SWEEPS - 1, SWEEPS - 4, -1):
            prepare(sweep)
    sums = [[None] * 2 for half in halves]
    for i in range(BAND):
        for half in halves:
            add(sums[half], i, entry(half, SWEEPS - 1, i) * initial[half](SWEEPS - 1 + i))
    totals = [add_up(terms) for terms in sums]
    for sweep in range(SWEEPS - 1, 0, -1):
        at = sweep + BAND - 1
        lasts = [before(half, sweep, at) - entry(half, sweep, BAND - 1) * totals[half] for half in halves]
        firsts = [
            jnp.where(heads[half], rows, pltpu.roll(lasts[half], 1, 1))
            for half, rows in enumerate(entering(sweep, lasts))
        ]
        for half in halves:
            states[half][at] = lasts[half]
            states[half][sweep - 1] = firsts[half]
        if prepare and sweep >= 3:
            prepare(sweep - 3)
        sums = [[None] * 2 for half in halves]
        for i in range(BAND - 1):
            for half in halves:
                row = before(half, sweep, sweep + i) - entry(half, sweep, i) * totals[half]
                states[half][sweep + i] = row
                add(sums[half], i, entry(half, sweep - 1, i + 1) * row)
        totals = [add_up(sums[half]) + entry(half, sweep - 1, 0) * firsts[half] for half in halves]
    for i in range(BAND):
        for half in halves:
            results[half][i] = states[half][i] - entry(half, 0, i) * totals[half]


def rows_of(tiles_ref, after_ref, half):
    return lambda i: tiles_ref[half, i] if i < BAND else after_ref[half, i - BAND]


def after_kernel(tiles_ref, halo_ref, after_ref, own_ref, gathered_ref):
    place, own_rows = lane_ids() % HALF, jnp.zeros(TILE, jnp.float32)
    for i in range(SWEEPS - 1):
        own_rows = jnp.where(place == i, pltpu.roll(tiles_ref[0, i], i, 1) if i else tiles_ref[0, 0], own_rows)
    own_ref[...] = own_rows
    last = lane_ids() % HALF == HALF - 1
    gathered_ref[...] = jnp.zeros_like(gathered_ref)
    gathered_ref[:HALF, :] = halo_ref[...]
    turned = gathered_ref[...].T
    slot = lane_ids() // HALF
    halo = turned[:HALF]
    for g in range(1, 8):
        halo = jnp.where(slot == g, pltpu.roll(turned[HALF * g : HALF * (g + 1)], HALF * g, 1), halo)
    for i in range(SWEEPS - 1):
        own = [pltpu.roll(tiles_ref[half, i], LANES - 1, 1) for half in range(2)]
        after_ref[0, i] = jnp.where(last, pltpu.roll(tiles_ref[1, i], HALF - 1, 1), own[0])
        after_ref[1, i] = jnp.where(last, pltpu.roll(halo, HALF - 1 - i, 1), own[1])


def rows_following(tiles, halo):
    return pl.pallas_call(
        after_kernel,
        out_shape=(
            jax.ShapeDtypeStruct((2, SWEEPS - 1) + TILE, jnp.float32),
            jax.ShapeDtypeStruct(TILE, jnp.float32),
        ),
        scratch_shapes=[pltpu.VMEM((LANES, LANES), jnp.float32)],
        name="after",
        compiler_params=PARAMS,
    )(tiles, halo)


def with_units(rows):
    zeros = jnp.zeros((8, LANES), jnp.float32)
    return lambda i: jnp.concatenate([rows(i), zeros], axis=0)


def unit(sweep):
    i, wide = sweep - 1, (24, LANES)
    row, parity = lax.broadcasted_iota(jnp.int32, wide, 0), lane_ids(wide) // HALF % 2
    return jnp.where(jnp.logical_and(row == 16 + i % 8, parity == i // 8), 1.0, 0.0)


def leave_kernel(
    tiles_ref, vectors_ref, after_ref,
    leaving_ref, lower_done_ref, upper_done_ref,
    lower_ref, upper_ref, lower_spread_ref, upper_spread_ref,
):
    rows = [rows_of(tiles_ref, after_ref, half) for half in range(2)]
    spreads = lower_spread_ref, upper_spread_ref

    def prepare(sweep):
        for half in range(2):
            for b, tile in enumerate(spread(vectors_ref, half, sweep)):
                spreads[half][sweep, 8 * b : 8 * (b + 1), :] = tile

    sweep_all(
        (lower_ref, upper_ref),
        spreads,
        (with_units(rows[0]), rows[1]),
        lambda sweep, lasts: (unit(sweep), pltpu.roll(lasts[0][:16], LANES - HALF + 1, 1)),
        prepare,
        (lower_done_ref, upper_done_ref),
    )
    leaving_ref[...] = rows_after(upper_ref)


STATE, WIDE, SPREAD = (BAND + SWEEPS,) + TILE, (BAND + SWEEPS, 24, LANES), (SWEEPS, BAND, LANES)
OCTS = (8, LANES, LANES)
OUT = (2 * HALF, BAND, LANES)
VMEM, ANY = pl.BlockSpec(memory_space=pltpu.VMEM), pl.BlockSpec(memory_space=pl.ANY)


def leave(tiles, vectors, after):
    shapes = TILE, (BAND, 24, LANES), (BAND,) + TILE
    return pl.pallas_call(
        leave_kernel,
        out_shape=tuple(jax.ShapeDtypeStruct(shape, jnp.float32) for shape in shapes),
        scratch_shapes=[pltpu.VMEM(shape, jnp.float32) for shape in (WIDE, STATE, SPREAD, SPREAD)],
        name="leave",
        compiler_params=PARAMS,
    )(tiles, vectors, after)


def upper_kernel(lower_ref, upper_ref, out_ref, fixed_ref, response_ref, rows_ref, sent):
    copies = []
    for o in range(8):
        turned = jnp.concatenate(swap_slots([upper_ref[8 * o + b] for b in range(8)]), axis=0)
        copies.append(turn_back(turned, rows_ref, out_ref, 1, o, sent))
    slot = lane_ids((8, LANES)) // HALF
    for o in range(8):
        fixed_ref[o] = jnp.concatenate(swap_slots([lower_ref[8 * o + b, :16, :] for b in range(8)]), axis=0)
        first, second = None, None
        for b in range(8):
            one = lower_ref[8 * o + b, 16:, :]
            parts = one, pltpu.roll(one, HALF, 1)
            first = parts[0] if first is None else jnp.where(slot == b, parts[b % 2], first)
            second = parts[1] if second is None else jnp.where(slot == b, parts[1 - b % 2], second)
        response_ref[o, :8, :] = first
        response_ref[o, 8:, :] = second
    for copy in copies:
        copy.wait()


def upper(*operands):
    return pl.pallas_call(
        upper_kernel,
        out_shape=tuple(jax.ShapeDtypeStruct(shape, jnp.float32) for shape in (OUT, OCTS, (8,) + TILE)),
        out_specs=(ANY, VMEM, VMEM),
        scratch_shapes=[pltpu.VMEM(OCTS, jnp.float32), pltpu.SemaphoreType.DMA((8,))],
        name="upper",
        compiler_params=PARAMS,
    )(*operands)


def lower_kernel(fixed_ref, response_ref, entering_ref, own_ref, upper_ref, out_ref, rows_ref, sent):
    tile = jnp.where(lax.axis_index("row") == 0, own_ref[...], entering_ref[...])
    entering = jnp.concatenate(
        [tile] + [pltpu.roll(tile, LANES - HALF * g, 1) for g in range(1, 8)], axis=0
    )[:, :HALF]
    copies = []
    for o in range(8):
        added = lax.dot_general(
            entering,
            response_ref[o],
            (((1,), (0,)), ((), ())),
            precision=lax.Precision.HIGHEST,
            preferred_element_type=jnp.float32,
        )
        copies.append(turn_back(fixed_ref[o] + added, rows_ref, out_ref, 0, o, sent))
    for copy in copies:
        copy.wait()


def lower(fixed, response, entering, own, upper_rows):
    return pl.pallas_call(
        lower_kernel,
        out_shape=jax.ShapeDtypeStruct(OUT, jnp.float32),
        in_specs=[VMEM] * 4 + [ANY],
        out_specs=ANY,
        scratch_shapes=[pltpu.VMEM(OCTS, jnp.float32), pltpu.SemaphoreType.DMA((8,))],
        input_output_aliases={4: 0},
        name="lower",
        compiler_params=PARAMS,
    )(fixed, response, entering, own, upper_rows)


def neighbour(value, step):
    owners = range(lax.axis_size("row"))
    return lax.ppermute(value, "row", [(i, i + step) for i in owners if i + step in owners])


def local(eigvecs, reflectors):
    vectors = lax.all_to_all(pack(reflectors), "col", 0, 0, tiled=True)
    halo = neighbour(eigvecs[:SWEEPS], -1)
    return sweeps(eigvecs, halo, vectors)


def sweeps(eigvecs, halo, vectors):
    tiles = turn(eigvecs)
    after, own = rows_following(tiles, halo)
    leaving, *done = leave(tiles, vectors, after)
    entering = neighbour(leaving, 1)
    upper_rows, fixed, response = upper(*done)
    return lower(fixed, response, entering, own, upper_rows).reshape(eigvecs.shape)


def solution(mesh):
    return jax.shard_map(
        local,
        mesh=mesh,
        in_specs=(P("row", "col"), P("col", "row", None)),
        out_specs=P("row", "col"),
        check_vma=False,
    )
```

```python
import jax
import jax.numpy as jnp
from jax import lax
from jax.experimental import pallas as pl
from jax.experimental.pallas import tpu as pltpu
from jax.sharding import PartitionSpec as P

SWEEPS, BAND, HALF, LANES = 16, 64, 16, 128
TILE = (16, 128)
PARAMS = pltpu.CompilerParams(vmem_limit_bytes=8 * 2**20)


def lane_ids(shape=TILE):
    return lax.broadcasted_iota(jnp.int32, shape, len(shape) - 1)


def shear(tiles):
    slot = lane_ids(tiles[0].shape) // HALF
    for s in (1, 2, 4):
        moved = slot & s != 0
        tiles = [jnp.where(moved, tiles[(t - s) % 8], tiles[t]) for t in range(8)]
    return tiles


def swap_slots(tiles):
    tiles = shear([tiles[-t % 8] for t in range(8)])
    return shear([pltpu.roll(tiles[t], LANES - HALF * t, 1) if t else tiles[t] for t in range(8)])


def pack_kernel(reflectors_ref, copies_ref, turned_ref):
    vectors = reflectors_ref[0]
    first = lax.broadcasted_iota(jnp.int32, vectors.shape, 1) == 0
    vectors = jnp.where(first, jnp.ones_like(vectors), vectors)
    vectors = vectors * jnp.sqrt(2.0 / jnp.sum(vectors * vectors, axis=1, keepdims=True))
    padded = jnp.concatenate([vectors, jnp.zeros_like(vectors)], axis=1)
    padded = jnp.concatenate([padded] + [jnp.zeros_like(padded)] * 3, axis=0)
    turned_ref[...] = padded.T
    slot = lane_ids((8, LANES)) // HALF
    for half in range(2):
        packed = jnp.zeros((8, LANES), jnp.float32)
        for b in range(8):
            entries = turned_ref[pl.ds(b, 8, stride=8), :]
            entries = pltpu.roll(entries, (HALF * (b - half)) % LANES, 1)
            packed = jnp.where(slot == b, entries, packed)
        for sweep in range(SWEEPS):
            copies_ref[sweep, 8 * half : 8 * (half + 1), :] = packed


def pack(reflectors):
    return pl.pallas_call(
        pack_kernel,
        out_shape=jax.ShapeDtypeStruct((SWEEPS, 16, LANES), jnp.float32),
        scratch_shapes=[pltpu.VMEM((LANES, LANES), jnp.float32)],
        name="pack",
        compiler_params=PARAMS,
    )(reflectors)


def turn_kernel(rows_ref, tiles_ref, gathered_ref):
    for half in range(2):
        for o in range(8):
            for b in range(8):
                gathered_ref[half, o, HALF * b : HALF * (b + 1), :] = rows_ref[
                    pl.ds(half * HALF * BAND + 8 * o + b, HALF, stride=BAND), :
                ]
            turned = gathered_ref[half, o].T
            tiles = swap_slots([turned[HALF * g : HALF * (g + 1)] for g in range(8)])
            for b in range(8):
                tiles_ref[half, 8 * o + b] = tiles[b]


def turn(rows):
    return pl.pallas_call(
        turn_kernel,
        out_shape=jax.ShapeDtypeStruct((2, BAND) + TILE, jnp.float32),
        scratch_shapes=[pltpu.VMEM((2, 8, LANES, LANES), jnp.float32)],
        name="turn",
        compiler_params=PARAMS,
    )(rows)


def turn_back(turned, rows_ref, out_ref, half, o, sent):
    rows = turned.T
    for b in range(8):
        rows_ref[o, pl.ds(b, HALF, stride=8), :] = rows[HALF * b : HALF * (b + 1)]
    copy = pltpu.make_async_copy(
        rows_ref.at[o].reshape(HALF, 8, LANES),
        out_ref.at[pl.ds(HALF * half, HALF), pl.ds(8 * o, 8)],
        sent.at[o],
    )
    copy.start()
    return copy


def rows_after(state_ref):
    place = lane_ids() % HALF
    tile = jnp.zeros(TILE, jnp.float32)
    for i in range(SWEEPS - 1):
        tile = jnp.where(place == i, pltpu.roll(state_ref[BAND + i], (i - HALF + 1) % LANES, 1), tile)
    return tile


def spread(vectors_ref, half, sweep):
    packed = vectors_ref[sweep, 8 * half : 8 * (half + 1), :]
    return shear([pltpu.roll(packed, LANES - HALF * t, 1) if t else packed for t in range(8)])


def add_up(terms):
    while len(terms) > 1:
        terms = [sum(terms[t + 1 : t + 2], terms[t]) for t in range(0, len(terms), 2)]
    return terms[0]


def sweep_all(states, spreads, initial, entering, prepare, results, ways=2):
    tiles = [state.shape[1:] for state in states]
    heads = [lane_ids(tile) % HALF == 0 for tile in tiles]
    halves = range(len(states))

    def entry(half, sweep, i):
        at = 8 * (i % 8) + i // 8
        return jnp.broadcast_to(spreads[half][sweep, at : at + 1, :], tiles[half])

    def before(half, sweep, i):
        return initial[half](i) if sweep == SWEEPS - 1 else states[half][i]

    def add(sums, i, term):
        sums[i % ways] = term if sums[i % ways] is None else sums[i % ways] + term

    if prepare:
        for sweep in range(SWEEPS - 1, SWEEPS - 4, -1):
            prepare(sweep)
    sums = [[None] * ways for half in halves]
    for i in range(BAND):
        for half in halves:
            add(sums[half], i, entry(half, SWEEPS - 1, i) * initial[half](SWEEPS - 1 + i))
    totals = [add_up(terms) for terms in sums]
    for sweep in range(SWEEPS - 1, 0, -1):
        at = sweep + BAND - 1
        lasts = [before(half, sweep, at) - entry(half, sweep, BAND - 1) * totals[half] for half in halves]
        firsts = [
            jnp.where(heads[half], rows, pltpu.roll(lasts[half], 1, 1))
            for half, rows in enumerate(entering(sweep, lasts))
        ]
        for half in halves:
            states[half][at] = lasts[half]
            states[half][sweep - 1] = firsts[half]
        if prepare and sweep >= 3:
            prepare(sweep - 3)
        sums = [[None] * ways for half in halves]
        for i in range(BAND - 1):
            for half in halves:
                row = before(half, sweep, sweep + i) - entry(half, sweep, i) * totals[half]
                states[half][sweep + i] = row
                add(sums[half], i, entry(half, sweep - 1, i + 1) * row)
        totals = [add_up(sums[half]) + entry(half, sweep - 1, 0) * firsts[half] for half in halves]
    for i in range(BAND):
        for half in halves:
            results[half][i] = states[half][i] - entry(half, 0, i) * totals[half]


def rows_of(tiles_ref, after_ref, half):
    return lambda i: tiles_ref[half, i] if i < BAND else after_ref[half, i - BAND]


def after_kernel(tiles_ref, halo_ref, after_ref, own_ref, gathered_ref):
    place, own_rows = lane_ids() % HALF, jnp.zeros(TILE, jnp.float32)
    for i in range(SWEEPS - 1):
        own_rows = jnp.where(place == i, pltpu.roll(tiles_ref[0, i], i, 1) if i else tiles_ref[0, 0], own_rows)
    own_ref[...] = own_rows
    last = lane_ids() % HALF == HALF - 1
    gathered_ref[...] = jnp.zeros_like(gathered_ref)
    gathered_ref[:HALF, :] = halo_ref[...]
    turned = gathered_ref[...].T
    slot = lane_ids() // HALF
    halo = turned[:HALF]
    for g in range(1, 8):
        halo = jnp.where(slot == g, pltpu.roll(turned[HALF * g : HALF * (g + 1)], HALF * g, 1), halo)
    for i in range(SWEEPS - 1):
        own = [pltpu.roll(tiles_ref[half, i], LANES - 1, 1) for half in range(2)]
        after_ref[0, i] = jnp.where(last, pltpu.roll(tiles_ref[1, i], HALF - 1, 1), own[0])
        after_ref[1, i] = jnp.where(last, pltpu.roll(halo, HALF - 1 - i, 1), own[1])


def rows_following(tiles, halo):
    return pl.pallas_call(
        after_kernel,
        out_shape=(
            jax.ShapeDtypeStruct((2, SWEEPS - 1) + TILE, jnp.float32),
            jax.ShapeDtypeStruct(TILE, jnp.float32),
        ),
        scratch_shapes=[pltpu.VMEM((LANES, LANES), jnp.float32)],
        name="after",
        compiler_params=PARAMS,
    )(tiles, halo)


def leave_kernel(
    tiles_ref, vectors_ref, after_ref,
    leaving_ref, lower_done_ref, upper_done_ref, spread_done_ref,
    lower_ref, upper_ref, lower_spread_ref, upper_spread_ref,
):
    zeros = jnp.zeros(TILE, jnp.float32)
    rows = [rows_of(tiles_ref, after_ref, half) for half in range(2)]
    spreads = lower_spread_ref, upper_spread_ref

    def prepare(sweep):
        for half in range(2):
            for b, tile in enumerate(spread(vectors_ref, half, sweep)):
                spreads[half][sweep, 8 * b : 8 * (b + 1), :] = tile
                if half == 0:
                    spread_done_ref[sweep, 8 * b : 8 * (b + 1), :] = tile

    sweep_all(
        (lower_ref, upper_ref),
        spreads,
        rows,
        lambda sweep, lasts: (zeros, pltpu.roll(lasts[0], LANES - HALF + 1, 1)),
        prepare,
        (lower_done_ref, upper_done_ref),
    )
    leaving_ref[...] = rows_after(upper_ref)


STATE, WIDE, SPREAD = (BAND + SWEEPS,) + TILE, (BAND + SWEEPS, 24, LANES), (SWEEPS, BAND, LANES)
OCTS = (8, LANES, LANES)
OUT = (2 * HALF, BAND, LANES)
VMEM, ANY = pl.BlockSpec(memory_space=pltpu.VMEM), pl.BlockSpec(memory_space=pl.ANY)


def leave(tiles, vectors, after):
    shapes = TILE, (BAND,) + TILE, (BAND,) + TILE, SPREAD
    return pl.pallas_call(
        leave_kernel,
        out_shape=tuple(jax.ShapeDtypeStruct(shape, jnp.float32) for shape in shapes),
        scratch_shapes=[pltpu.VMEM(shape, jnp.float32) for shape in (STATE, STATE, SPREAD, SPREAD)],
        name="leave",
        compiler_params=PARAMS,
    )(tiles, vectors, after)


def unit_sweeps(spread_ref, unit_ref, gaps):
    tile = (8, LANES)
    row, lane = lax.broadcasted_iota(jnp.int32, tile, 0), lane_ids(tile)
    zeros = jnp.zeros(tile, jnp.float32)

    def entering(sweep, lasts):
        i = sweep - 1
        gaps(sweep)
        return (jnp.where(jnp.logical_and(row == i % 8, lane // HALF % 2 == i // 8), 1.0, 0.0),)

    sweep_all((unit_ref,), (spread_ref,), (lambda i: zeros,), entering, None, (unit_ref,), 4)


def upper_kernel(lower_ref, upper_ref, spread_ref, out_ref, fixed_ref, response_ref, rows_ref, sent, unit_ref):
    copies = []

    def gaps(sweep):
        if sweep % 2:
            o = 7 - sweep // 2
            turned = jnp.concatenate(swap_slots([upper_ref[8 * o + b] for b in range(8)]), axis=0)
            copies.append(turn_back(turned, rows_ref, out_ref, 1, o, sent))

    unit_sweeps(spread_ref, unit_ref, gaps)
    slot = lane_ids((8, LANES)) // HALF
    for o in range(8):
        fixed_ref[o] = jnp.concatenate(swap_slots([lower_ref[8 * o + b] for b in range(8)]), axis=0)
        first, second = None, None
        for b in range(8):
            one = unit_ref[8 * o + b]
            parts = one, pltpu.roll(one, HALF, 1)
            first = parts[0] if first is None else jnp.where(slot == b, parts[b % 2], first)
            second = parts[1] if second is None else jnp.where(slot == b, parts[1 - b % 2], second)
        response_ref[o, :8, :] = first
        response_ref[o, 8:, :] = second
    for copy in copies:
        copy.wait()


def upper(*operands):
    return pl.pallas_call(
        upper_kernel,
        out_shape=tuple(jax.ShapeDtypeStruct(shape, jnp.float32) for shape in (OUT, OCTS, (8,) + TILE)),
        out_specs=(ANY, VMEM, VMEM),
        scratch_shapes=[
            pltpu.VMEM(OCTS, jnp.float32),
            pltpu.SemaphoreType.DMA((8,)),
            pltpu.VMEM((BAND + SWEEPS, 8, LANES), jnp.float32),
        ],
        name="upper",
        compiler_params=PARAMS,
    )(*operands)


def in_parts(values):
    high = values.astype(jnp.bfloat16)
    return high, (values - high.astype(jnp.float32)).astype(jnp.bfloat16)


def product(a, b):
    return jnp.dot(a, b, preferred_element_type=jnp.float32)


def lower_kernel(fixed_ref, response_ref, entering_ref, own_ref, upper_ref, out_ref, rows_ref, sent):
    tile = jnp.where(lax.axis_index("row") == 0, own_ref[...], entering_ref[...])
    entering = jnp.concatenate(
        [tile] + [pltpu.roll(tile, LANES - HALF * g, 1) for g in range(1, 8)], axis=0
    )[:, :HALF]
    entering_high, entering_low = in_parts(entering)
    copies = []
    for o in range(8):
        high, low = in_parts(response_ref[o])
        added = product(entering_high, high) + (product(entering_low, high) + product(entering_high, low))
        copies.append(turn_back(fixed_ref[o] + added, rows_ref, out_ref, 0, o, sent))
    for copy in copies:
        copy.wait()


def lower(fixed, response, entering, own, upper_rows):
    return pl.pallas_call(
        lower_kernel,
        out_shape=jax.ShapeDtypeStruct(OUT, jnp.float32),
        in_specs=[VMEM] * 4 + [ANY],
        out_specs=ANY,
        scratch_shapes=[pltpu.VMEM(OCTS, jnp.float32), pltpu.SemaphoreType.DMA((8,))],
        input_output_aliases={4: 0},
        name="lower",
        compiler_params=PARAMS,
    )(fixed, response, entering, own, upper_rows)


def neighbour(value, step):
    owners = range(lax.axis_size("row"))
    return lax.ppermute(value, "row", [(i, i + step) for i in owners if i + step in owners])


def local(eigvecs, reflectors):
    vectors = lax.all_to_all(pack(reflectors), "col", 0, 0, tiled=True)
    halo = neighbour(eigvecs[:SWEEPS], -1)
    return sweeps(eigvecs, halo, vectors)


def sweeps(eigvecs, halo, vectors):
    tiles = turn(eigvecs)
    after, own = rows_following(tiles, halo)
    leaving, *done = leave(tiles, vectors, after)
    entering = neighbour(leaving, 1)
    upper_rows, fixed, response = upper(*done)
    return lower(fixed, response, entering, own, upper_rows).reshape(eigvecs.shape)


def solution(mesh):
    return jax.shard_map(
        local,
        mesh=mesh,
        in_specs=(P("row", "col"), P("col", "row", None)),
        out_specs=P("row", "col"),
        check_vma=False,
    )
```

```python
import jax
import jax.numpy as jnp
from jax import lax
from jax.experimental import pallas as pl
from jax.experimental.pallas import tpu as pltpu
from jax.sharding import PartitionSpec as P

SWEEPS, BAND, HALF, LANES = 16, 64, 16, 128
TILE = (16, 128)
PARAMS = pltpu.CompilerParams(vmem_limit_bytes=8 * 2**20)


def lane_ids(shape=TILE):
    return lax.broadcasted_iota(jnp.int32, shape, len(shape) - 1)


def shear(tiles):
    slot = lane_ids(tiles[0].shape) // HALF
    for s in (1, 2, 4):
        moved = slot & s != 0
        tiles = [jnp.where(moved, tiles[(t - s) % 8], tiles[t]) for t in range(8)]
    return tiles


def swap_slots(tiles):
    tiles = shear([tiles[-t % 8] for t in range(8)])
    return shear([pltpu.roll(tiles[t], LANES - HALF * t, 1) if t else tiles[t] for t in range(8)])


def pack_kernel(reflectors_ref, copies_ref, turned_ref):
    vectors = reflectors_ref[0]
    first = lax.broadcasted_iota(jnp.int32, vectors.shape, 1) == 0
    vectors = jnp.where(first, jnp.ones_like(vectors), vectors)
    vectors = vectors * jnp.sqrt(2.0 / jnp.sum(vectors * vectors, axis=1, keepdims=True))
    padded = jnp.concatenate([vectors, jnp.zeros_like(vectors)], axis=1)
    padded = jnp.concatenate([padded] + [jnp.zeros_like(padded)] * 3, axis=0)
    turned_ref[...] = padded.T
    slot = lane_ids((8, LANES)) // HALF
    for half in range(2):
        packed = jnp.zeros((8, LANES), jnp.float32)
        for b in range(8):
            entries = turned_ref[pl.ds(b, 8, stride=8), :]
            entries = pltpu.roll(entries, (HALF * (b - half)) % LANES, 1)
            packed = jnp.where(slot == b, entries, packed)
        for sweep in range(SWEEPS):
            copies_ref[sweep, 8 * half : 8 * (half + 1), :] = packed


def pack(reflectors):
    return pl.pallas_call(
        pack_kernel,
        out_shape=jax.ShapeDtypeStruct((SWEEPS, 16, LANES), jnp.float32),
        scratch_shapes=[pltpu.VMEM((LANES, LANES), jnp.float32)],
        name="pack",
        compiler_params=PARAMS,
    )(reflectors)


def turn_kernel(rows_ref, tiles_ref, gathered_ref):
    for half in range(2):
        for o in range(8):
            for b in range(8):
                gathered_ref[half, o, HALF * b : HALF * (b + 1), :] = rows_ref[
                    pl.ds(half * HALF * BAND + 8 * o + b, HALF, stride=BAND), :
                ]
            turned = gathered_ref[half, o].T
            tiles = swap_slots([turned[HALF * g : HALF * (g + 1)] for g in range(8)])
            for b in range(8):
                tiles_ref[half, 8 * o + b] = tiles[b]


def turn(rows):
    return pl.pallas_call(
        turn_kernel,
        out_shape=jax.ShapeDtypeStruct((2, BAND) + TILE, jnp.float32),
        scratch_shapes=[pltpu.VMEM((2, 8, LANES, LANES), jnp.float32)],
        name="turn",
        compiler_params=PARAMS,
    )(rows)


def turn_back(turned, rows_ref, out_ref, half, o, sent):
    rows = turned.T
    for b in range(8):
        rows_ref[o, pl.ds(b, HALF, stride=8), :] = rows[HALF * b : HALF * (b + 1)]
    copy = pltpu.make_async_copy(
        rows_ref.at[o].reshape(HALF, 8, LANES),
        out_ref.at[pl.ds(HALF * half, HALF), pl.ds(8 * o, 8)],
        sent.at[o],
    )
    copy.start()
    return copy


def rows_after(state_ref):
    place = lane_ids() % HALF
    tile = jnp.zeros(TILE, jnp.float32)
    for i in range(SWEEPS - 1):
        tile = jnp.where(place == i, pltpu.roll(state_ref[BAND + i], (i - HALF + 1) % LANES, 1), tile)
    return tile


def spread(vectors_ref, half, sweep):
    packed = vectors_ref[sweep, 8 * half : 8 * (half + 1), :]
    return shear([pltpu.roll(packed, LANES - HALF * t, 1) if t else packed for t in range(8)])


def add_up(terms):
    while len(terms) > 1:
        terms = [sum(terms[t + 1 : t + 2], terms[t]) for t in range(0, len(terms), 2)]
    return terms[0]


def sweep_all(states, spreads, initial, entering, prepare, results, ways=2, final=0):
    tiles = [state.shape[1:] for state in states]
    heads = [lane_ids(tile) % HALF == 0 for tile in tiles]
    halves = range(len(states))

    def entry(half, sweep, i):
        at = 8 * (i % 8) + i // 8
        return jnp.broadcast_to(spreads[half][sweep, at : at + 1, :], tiles[half])

    def before(half, sweep, i):
        return initial[half](i) if sweep == SWEEPS - 1 else states[half][i]

    def add(sums, i, term):
        sums[i % ways] = term if sums[i % ways] is None else sums[i % ways] + term

    if prepare:
        for sweep in range(SWEEPS - 1, SWEEPS - 4, -1):
            prepare(sweep)
    sums = [[None] * ways for half in halves]
    for i in range(BAND):
        for half in halves:
            add(sums[half], i, entry(half, SWEEPS - 1, i) * initial[half](SWEEPS - 1 + i))
    totals = [add_up(terms) for terms in sums]
    for sweep in range(SWEEPS - 1, 0, -1):
        at = sweep + BAND - 1
        lasts = [before(half, sweep, at) - entry(half, sweep, BAND - 1) * totals[half] for half in halves]
        firsts = [
            jnp.where(heads[half], rows, pltpu.roll(lasts[half], 1, 1))
            for half, rows in enumerate(entering(sweep, lasts))
        ]
        for half in halves:
            states[half][at] = lasts[half]
            states[half][sweep - 1] = firsts[half]
        if prepare and sweep >= 3:
            prepare(sweep - 3)
        sums = [[None] * ways for half in halves]
        for i in range(BAND - 1):
            for half in halves:
                row = before(half, sweep, sweep + i) - entry(half, sweep, i) * totals[half]
                if sweep == final:
                    results[half][sweep + i] = row
                    continue
                states[half][sweep + i] = row
                add(sums[half], i, entry(half, sweep - 1, i + 1) * row)
        if sweep == final:
            for half in halves:
                results[half][0] = firsts[half]
            return
        totals = [add_up(sums[half]) + entry(half, sweep - 1, 0) * firsts[half] for half in halves]
    for i in range(BAND):
        for half in halves:
            results[half][i] = states[half][i] - entry(half, 0, i) * totals[half]


def rows_of(tiles_ref, after_ref, half):
    return lambda i: tiles_ref[half, i] if i < BAND else after_ref[half, i - BAND]


def after_kernel(tiles_ref, halo_ref, after_ref, own_ref, gathered_ref):
    place, own_rows = lane_ids() % HALF, jnp.zeros(TILE, jnp.float32)
    for i in range(SWEEPS - 1):
        own_rows = jnp.where(place == i, pltpu.roll(tiles_ref[0, i], i, 1) if i else tiles_ref[0, 0], own_rows)
    own_ref[...] = own_rows
    last = lane_ids() % HALF == HALF - 1
    gathered_ref[...] = jnp.zeros_like(gathered_ref)
    gathered_ref[:HALF, :] = halo_ref[...]
    turned = gathered_ref[...].T
    slot = lane_ids() // HALF
    halo = turned[:HALF]
    for g in range(1, 8):
        halo = jnp.where(slot == g, pltpu.roll(turned[HALF * g : HALF * (g + 1)], HALF * g, 1), halo)
    for i in range(SWEEPS - 1):
        own = [pltpu.roll(tiles_ref[half, i], LANES - 1, 1) for half in range(2)]
        after_ref[0, i] = jnp.where(last, pltpu.roll(tiles_ref[1, i], HALF - 1, 1), own[0])
        after_ref[1, i] = jnp.where(last, pltpu.roll(halo, HALF - 1 - i, 1), own[1])


def rows_following(tiles, halo):
    return pl.pallas_call(
        after_kernel,
        out_shape=(
            jax.ShapeDtypeStruct((2, SWEEPS - 1) + TILE, jnp.float32),
            jax.ShapeDtypeStruct(TILE, jnp.float32),
        ),
        scratch_shapes=[pltpu.VMEM((LANES, LANES), jnp.float32)],
        name="after",
        compiler_params=PARAMS,
    )(tiles, halo)


def leave_kernel(
    tiles_ref, vectors_ref, after_ref,
    leaving_ref, lower_done_ref, upper_done_ref, spread_done_ref,
    lower_ref, upper_ref, lower_spread_ref, upper_spread_ref,
):
    zeros = jnp.zeros(TILE, jnp.float32)
    rows = [rows_of(tiles_ref, after_ref, half) for half in range(2)]
    spreads = lower_spread_ref, upper_spread_ref

    def prepare(sweep):
        for half in range(2):
            for b, tile in enumerate(spread(vectors_ref, half, sweep)):
                spreads[half][sweep, 8 * b : 8 * (b + 1), :] = tile
                if half == 0:
                    spread_done_ref[sweep, 8 * b : 8 * (b + 1), :] = tile

    sweep_all(
        (lower_ref, upper_ref),
        spreads,
        rows,
        lambda sweep, lasts: (zeros, pltpu.roll(lasts[0], LANES - HALF + 1, 1)),
        prepare,
        (lower_done_ref, upper_done_ref),
        final=1,
    )
    leaving_ref[...] = rows_after(upper_ref)


STATE, WIDE, SPREAD = (BAND + SWEEPS,) + TILE, (BAND + SWEEPS, 24, LANES), (SWEEPS, BAND, LANES)
OCTS = (8, LANES, LANES)
OUT = (2 * HALF, BAND, LANES)
VMEM, ANY = pl.BlockSpec(memory_space=pltpu.VMEM), pl.BlockSpec(memory_space=pl.ANY)


def leave(tiles, vectors, after):
    shapes = TILE, (BAND,) + TILE, (BAND,) + TILE, SPREAD
    return pl.pallas_call(
        leave_kernel,
        out_shape=tuple(jax.ShapeDtypeStruct(shape, jnp.float32) for shape in shapes),
        scratch_shapes=[pltpu.VMEM(shape, jnp.float32) for shape in (STATE, STATE, SPREAD, SPREAD)],
        name="leave",
        compiler_params=PARAMS,
    )(tiles, vectors, after)


def unit_sweeps(spread_ref, unit_ref, gaps):
    tile = (8, LANES)
    row, lane = lax.broadcasted_iota(jnp.int32, tile, 0), lane_ids(tile)
    zeros = jnp.zeros(tile, jnp.float32)

    def entering(sweep, lasts):
        i = sweep - 1
        gaps(sweep)
        return (jnp.where(jnp.logical_and(row == i % 8, lane // HALF % 2 == i // 8), 1.0, 0.0),)

    sweep_all((unit_ref,), (spread_ref,), (lambda i: zeros,), entering, None, (unit_ref,), 4)


def last_sweep(state_ref, entry):
    sums = [None] * 4
    for i in range(BAND):
        term = entry(i) * state_ref[i]
        sums[i % 4] = term if sums[i % 4] is None else sums[i % 4] + term
    total = add_up(sums)
    return lambda i: state_ref[i] - entry(i) * total


def upper_kernel(
    lower_ref, upper_ref, spread_ref, vectors_ref,
    out_ref, fixed_ref, response_ref,
    rows_ref, sent, unit_ref, last_ref,
):
    for b, tile in enumerate(spread(vectors_ref, 1, 0)):
        last_ref[8 * b : 8 * (b + 1), :] = tile

    def row_at(ref, i):
        at = 8 * (i % 8) + i // 8
        return jnp.broadcast_to(ref[at : at + 1, :], TILE)

    upper_row = last_sweep(upper_ref, lambda i: row_at(last_ref, i))
    lower_row = last_sweep(lower_ref, lambda i: row_at(spread_ref.at[0], i))
    copies = []

    def gaps(sweep):
        if sweep % 2:
            o = 7 - sweep // 2
            turned = jnp.concatenate(swap_slots([upper_row(8 * o + b) for b in range(8)]), axis=0)
            copies.append(turn_back(turned, rows_ref, out_ref, 1, o, sent))

    unit_sweeps(spread_ref, unit_ref, gaps)
    slot = lane_ids((8, LANES)) // HALF
    for o in range(8):
        fixed_ref[o] = jnp.concatenate(swap_slots([lower_row(8 * o + b) for b in range(8)]), axis=0)
        first, second = None, None
        for b in range(8):
            one = unit_ref[8 * o + b]
            parts = one, pltpu.roll(one, HALF, 1)
            first = parts[0] if first is None else jnp.where(slot == b, parts[b % 2], first)
            second = parts[1] if second is None else jnp.where(slot == b, parts[1 - b % 2], second)
        response_ref[o, :8, :] = first
        response_ref[o, 8:, :] = second
    for copy in copies:
        copy.wait()


def upper(*operands):
    return pl.pallas_call(
        upper_kernel,
        out_shape=tuple(jax.ShapeDtypeStruct(shape, jnp.float32) for shape in (OUT, OCTS, (8,) + TILE)),
        out_specs=(ANY, VMEM, VMEM),
        scratch_shapes=[
            pltpu.VMEM(OCTS, jnp.float32),
            pltpu.SemaphoreType.DMA((8,)),
            pltpu.VMEM((BAND + SWEEPS, 8, LANES), jnp.float32),
            pltpu.VMEM((BAND, LANES), jnp.float32),
        ],
        name="upper",
        compiler_params=PARAMS,
    )(*operands)


def in_parts(values):
    high = values.astype(jnp.bfloat16)
    return high, (values - high.astype(jnp.float32)).astype(jnp.bfloat16)


def product(a, b):
    return jnp.dot(a, b, preferred_element_type=jnp.float32)


def lower_kernel(fixed_ref, response_ref, entering_ref, own_ref, upper_ref, out_ref, rows_ref, sent):
    tile = jnp.where(lax.axis_index("row") == 0, own_ref[...], entering_ref[...])
    entering = jnp.concatenate(
        [tile] + [pltpu.roll(tile, LANES - HALF * g, 1) for g in range(1, 8)], axis=0
    )[:, :HALF]
    entering_high, entering_low = in_parts(entering)
    copies = []
    for o in range(8):
        high, low = in_parts(response_ref[o])
        added = product(entering_high, high) + (product(entering_low, high) + product(entering_high, low))
        copies.append(turn_back(fixed_ref[o] + added, rows_ref, out_ref, 0, o, sent))
    for copy in copies:
        copy.wait()


def lower(fixed, response, entering, own, upper_rows):
    return pl.pallas_call(
        lower_kernel,
        out_shape=jax.ShapeDtypeStruct(OUT, jnp.float32),
        in_specs=[VMEM] * 4 + [ANY],
        out_specs=ANY,
        scratch_shapes=[pltpu.VMEM(OCTS, jnp.float32), pltpu.SemaphoreType.DMA((8,))],
        input_output_aliases={4: 0},
        name="lower",
        compiler_params=PARAMS,
    )(fixed, response, entering, own, upper_rows)


def neighbour(value, step):
    owners = range(lax.axis_size("row"))
    return lax.ppermute(value, "row", [(i, i + step) for i in owners if i + step in owners])


def local(eigvecs, reflectors):
    vectors = lax.all_to_all(pack(reflectors), "col", 0, 0, tiled=True)
    halo = neighbour(eigvecs[:SWEEPS], -1)
    return sweeps(eigvecs, halo, vectors)


def sweeps(eigvecs, halo, vectors):
    tiles = turn(eigvecs)
    after, own = rows_following(tiles, halo)
    leaving, *done = leave(tiles, vectors, after)
    entering = neighbour(leaving, 1)
    upper_rows, fixed, response = upper(*done, vectors)
    return lower(fixed, response, entering, own, upper_rows).reshape(eigvecs.shape)


def solution(mesh):
    return jax.shard_map(
        local,
        mesh=mesh,
        in_specs=(P("row", "col"), P("col", "row", None)),
        out_specs=P("row", "col"),
        check_vma=False,
    )
```

```python
import jax
import jax.numpy as jnp
from jax import lax
from jax.experimental import pallas as pl
from jax.experimental.pallas import tpu as pltpu
from jax.sharding import PartitionSpec as P

SWEEPS, BAND, HALF, LANES = 16, 64, 16, 128
TILE = (16, 128)
PARAMS = pltpu.CompilerParams(vmem_limit_bytes=8 * 2**20)


def lane_ids(shape=TILE):
    return lax.broadcasted_iota(jnp.int32, shape, len(shape) - 1)


def shear(tiles):
    slot = lane_ids(tiles[0].shape) // HALF
    for s in (1, 2, 4):
        moved = slot & s != 0
        tiles = [jnp.where(moved, tiles[(t - s) % 8], tiles[t]) for t in range(8)]
    return tiles


def swap_slots(tiles):
    tiles = shear([tiles[-t % 8] for t in range(8)])
    return shear([pltpu.roll(tiles[t], LANES - HALF * t, 1) if t else tiles[t] for t in range(8)])


def pack_kernel(reflectors_ref, copies_ref, turned_ref):
    vectors = reflectors_ref[0]
    first = lax.broadcasted_iota(jnp.int32, vectors.shape, 1) == 0
    vectors = jnp.where(first, jnp.ones_like(vectors), vectors)
    vectors = vectors * jnp.sqrt(2.0 / jnp.sum(vectors * vectors, axis=1, keepdims=True))
    padded = jnp.concatenate([vectors, jnp.zeros_like(vectors)], axis=1)
    padded = jnp.concatenate([padded] + [jnp.zeros_like(padded)] * 3, axis=0)
    turned_ref[...] = padded.T
    slot = lane_ids((8, LANES)) // HALF
    for half in range(2):
        packed = jnp.zeros((8, LANES), jnp.float32)
        for b in range(8):
            entries = turned_ref[pl.ds(b, 8, stride=8), :]
            entries = pltpu.roll(entries, (HALF * (b - half)) % LANES, 1)
            packed = jnp.where(slot == b, entries, packed)
        for sweep in range(SWEEPS):
            copies_ref[sweep, 8 * half : 8 * (half + 1), :] = packed


def pack(reflectors):
    return pl.pallas_call(
        pack_kernel,
        out_shape=jax.ShapeDtypeStruct((SWEEPS, 16, LANES), jnp.float32),
        scratch_shapes=[pltpu.VMEM((LANES, LANES), jnp.float32)],
        name="pack",
        compiler_params=pltpu.CompilerParams(vmem_limit_bytes=56 * 2**20),
    )(reflectors)


def turn_kernel(rows_ref, tiles_ref, gathered_ref):
    for half in range(2):
        for o in range(8):
            for b in range(8):
                gathered_ref[half, o, HALF * b : HALF * (b + 1), :] = rows_ref[
                    pl.ds(half * HALF * BAND + 8 * o + b, HALF, stride=BAND), :
                ]
            turned = gathered_ref[half, o].T
            tiles = swap_slots([turned[HALF * g : HALF * (g + 1)] for g in range(8)])
            for b in range(8):
                tiles_ref[half, 8 * o + b] = tiles[b]


def turn(rows):
    return pl.pallas_call(
        turn_kernel,
        out_shape=jax.ShapeDtypeStruct((2, BAND) + TILE, jnp.float32),
        scratch_shapes=[pltpu.VMEM((2, 8, LANES, LANES), jnp.float32)],
        name="turn",
        compiler_params=PARAMS,
    )(rows)


def turn_back(turned, rows_ref, out_ref, half, o, sent):
    rows = turned.T
    for b in range(8):
        rows_ref[o, pl.ds(b, HALF, stride=8), :] = rows[HALF * b : HALF * (b + 1)]
    copy = pltpu.make_async_copy(
        rows_ref.at[o].reshape(HALF, 8, LANES),
        out_ref.at[pl.ds(HALF * half, HALF), pl.ds(8 * o, 8)],
        sent.at[o],
    )
    copy.start()
    return copy


def rows_after(state_ref):
    place = lane_ids() % HALF
    tile = jnp.zeros(TILE, jnp.float32)
    for i in range(SWEEPS - 1):
        tile = jnp.where(place == i, pltpu.roll(state_ref[BAND + i], (i - HALF + 1) % LANES, 1), tile)
    return tile


def spread(vectors_ref, half, sweep):
    packed = vectors_ref[sweep, 8 * half : 8 * (half + 1), :]
    return shear([pltpu.roll(packed, LANES - HALF * t, 1) if t else packed for t in range(8)])


def add_up(terms):
    while len(terms) > 1:
        terms = [sum(terms[t + 1 : t + 2], terms[t]) for t in range(0, len(terms), 2)]
    return terms[0]


def sweep_all(states, spreads, initial, entering, prepare, results, ways=2):
    tiles = [state.shape[1:] for state in states]
    heads = [lane_ids(tile) % HALF == 0 for tile in tiles]
    halves = range(len(states))

    def entry(half, sweep, i):
        at = 8 * (i % 8) + i // 8
        return jnp.broadcast_to(spreads[half][sweep, at : at + 1, :], tiles[half])

    def before(half, sweep, i):
        return initial[half](i) if sweep == SWEEPS - 1 else states[half][i]

    def add(sums, i, term):
        sums[i % ways] = term if sums[i % ways] is None else sums[i % ways] + term

    if prepare:
        for sweep in range(SWEEPS - 1, SWEEPS - 4, -1):
            prepare(sweep)
    sums = [[None] * ways for half in halves]
    for i in range(BAND):
        for half in halves:
            add(sums[half], i, entry(half, SWEEPS - 1, i) * initial[half](SWEEPS - 1 + i))
    totals = [add_up(terms) for terms in sums]
    for sweep in range(SWEEPS - 1, 0, -1):
        at = sweep + BAND - 1
        lasts = [before(half, sweep, at) - entry(half, sweep, BAND - 1) * totals[half] for half in halves]
        firsts = [
            jnp.where(heads[half], rows, pltpu.roll(lasts[half], 1, 1))
            for half, rows in enumerate(entering(sweep, lasts))
        ]
        for half in halves:
            states[half][at] = lasts[half]
            states[half][sweep - 1] = firsts[half]
        if prepare and sweep >= 3:
            prepare(sweep - 3)
        sums = [[None] * ways for half in halves]
        for i in range(BAND - 1):
            for half in halves:
                row = before(half, sweep, sweep + i) - entry(half, sweep, i) * totals[half]
                states[half][sweep + i] = row
                add(sums[half], i, entry(half, sweep - 1, i + 1) * row)
        totals = [add_up(sums[half]) + entry(half, sweep - 1, 0) * firsts[half] for half in halves]
    for i in range(BAND):
        for half in halves:
            results[half][i] = states[half][i] - entry(half, 0, i) * totals[half]


def rows_of(tiles_ref, after_ref, half):
    return lambda i: tiles_ref[half, i] if i < BAND else after_ref[half, i - BAND]


def after_kernel(tiles_ref, halo_ref, after_ref, own_ref, gathered_ref):
    place, own_rows = lane_ids() % HALF, jnp.zeros(TILE, jnp.float32)
    for i in range(SWEEPS - 1):
        own_rows = jnp.where(place == i, pltpu.roll(tiles_ref[0, i], i, 1) if i else tiles_ref[0, 0], own_rows)
    own_ref[...] = own_rows
    last = lane_ids() % HALF == HALF - 1
    gathered_ref[...] = jnp.zeros_like(gathered_ref)
    gathered_ref[:HALF, :] = halo_ref[...]
    turned = gathered_ref[...].T
    slot = lane_ids() // HALF
    halo = turned[:HALF]
    for g in range(1, 8):
        halo = jnp.where(slot == g, pltpu.roll(turned[HALF * g : HALF * (g + 1)], HALF * g, 1), halo)
    for i in range(SWEEPS - 1):
        own = [pltpu.roll(tiles_ref[half, i], LANES - 1, 1) for half in range(2)]
        after_ref[0, i] = jnp.where(last, pltpu.roll(tiles_ref[1, i], HALF - 1, 1), own[0])
        after_ref[1, i] = jnp.where(last, pltpu.roll(halo, HALF - 1 - i, 1), own[1])


def rows_following(tiles, halo):
    return pl.pallas_call(
        after_kernel,
        out_shape=(
            jax.ShapeDtypeStruct((2, SWEEPS - 1) + TILE, jnp.float32),
            jax.ShapeDtypeStruct(TILE, jnp.float32),
        ),
        scratch_shapes=[pltpu.VMEM((LANES, LANES), jnp.float32)],
        name="after",
        compiler_params=PARAMS,
    )(tiles, halo)


def leave_kernel(
    tiles_ref, vectors_ref, after_ref,
    leaving_ref, lower_done_ref, upper_done_ref, spread_done_ref,
    lower_ref, upper_ref, lower_spread_ref, upper_spread_ref,
):
    zeros = jnp.zeros(TILE, jnp.float32)
    rows = [rows_of(tiles_ref, after_ref, half) for half in range(2)]
    spreads = lower_spread_ref, upper_spread_ref

    def prepare(sweep):
        for half in range(2):
            for b, tile in enumerate(spread(vectors_ref, half, sweep)):
                spreads[half][sweep, 8 * b : 8 * (b + 1), :] = tile
                if half == 0:
                    spread_done_ref[sweep, 8 * b : 8 * (b + 1), :] = tile

    sweep_all(
        (lower_ref, upper_ref),
        spreads,
        rows,
        lambda sweep, lasts: (zeros, pltpu.roll(lasts[0], LANES - HALF + 1, 1)),
        prepare,
        (lower_done_ref, upper_done_ref),
    )
    leaving_ref[...] = rows_after(upper_ref)


STATE, WIDE, SPREAD = (BAND + SWEEPS,) + TILE, (BAND + SWEEPS, 24, LANES), (SWEEPS, BAND, LANES)
OCTS = (8, LANES, LANES)
OUT = (2 * HALF, BAND, LANES)
VMEM, ANY = pl.BlockSpec(memory_space=pltpu.VMEM), pl.BlockSpec(memory_space=pl.ANY)


def leave(tiles, vectors, after):
    shapes = TILE, (BAND,) + TILE, (BAND,) + TILE, SPREAD
    return pl.pallas_call(
        leave_kernel,
        out_shape=tuple(jax.ShapeDtypeStruct(shape, jnp.float32) for shape in shapes),
        scratch_shapes=[pltpu.VMEM(shape, jnp.float32) for shape in (STATE, STATE, SPREAD, SPREAD)],
        name="leave",
        compiler_params=PARAMS,
    )(tiles, vectors, after)


def unit_sweeps(spread_ref, unit_ref, gaps):
    tile = (8, LANES)
    row, lane = lax.broadcasted_iota(jnp.int32, tile, 0), lane_ids(tile)
    zeros = jnp.zeros(tile, jnp.float32)

    def entering(sweep, lasts):
        i = sweep - 1
        gaps(sweep)
        return (jnp.where(jnp.logical_and(row == i % 8, lane // HALF % 2 == i // 8), 1.0, 0.0),)

    sweep_all((unit_ref,), (spread_ref,), (lambda i: zeros,), entering, None, (unit_ref,), 4)


def upper_kernel(lower_ref, upper_ref, spread_ref, out_ref, fixed_ref, response_ref, rows_ref, sent, unit_ref):
    copies = []

    def gaps(sweep):
        if sweep % 2:
            o = 7 - sweep // 2
            turned = jnp.concatenate(swap_slots([upper_ref[8 * o + b] for b in range(8)]), axis=0)
            copies.append(turn_back(turned, rows_ref, out_ref, 1, o, sent))

    unit_sweeps(spread_ref, unit_ref, gaps)
    slot = lane_ids((8, LANES)) // HALF
    for o in range(8):
        fixed_ref[o] = jnp.concatenate(swap_slots([lower_ref[8 * o + b] for b in range(8)]), axis=0)
        first, second = None, None
        for b in range(8):
            one = unit_ref[8 * o + b]
            parts = one, pltpu.roll(one, HALF, 1)
            first = parts[0] if first is None else jnp.where(slot == b, parts[b % 2], first)
            second = parts[1] if second is None else jnp.where(slot == b, parts[1 - b % 2], second)
        response_ref[o, :8, :] = first
        response_ref[o, 8:, :] = second
    for copy in copies:
        copy.wait()


def upper(*operands):
    return pl.pallas_call(
        upper_kernel,
        out_shape=tuple(jax.ShapeDtypeStruct(shape, jnp.float32) for shape in (OUT, OCTS, (8,) + TILE)),
        out_specs=(ANY, VMEM, VMEM),
        scratch_shapes=[
            pltpu.VMEM(OCTS, jnp.float32),
            pltpu.SemaphoreType.DMA((8,)),
            pltpu.VMEM((BAND + SWEEPS, 8, LANES), jnp.float32),
        ],
        name="upper",
        compiler_params=PARAMS,
    )(*operands)


def in_parts(values):
    high = values.astype(jnp.bfloat16)
    return high, (values - high.astype(jnp.float32)).astype(jnp.bfloat16)


def product(a, b):
    return jnp.dot(a, b, preferred_element_type=jnp.float32)


def lower_kernel(fixed_ref, response_ref, entering_ref, own_ref, upper_ref, out_ref, rows_ref, sent):
    tile = jnp.where(lax.axis_index("row") == 0, own_ref[...], entering_ref[...])
    entering = jnp.concatenate(
        [tile] + [pltpu.roll(tile, LANES - HALF * g, 1) for g in range(1, 8)], axis=0
    )[:, :HALF]
    entering_high, entering_low = in_parts(entering)
    copies = []
    for o in range(8):
        high, low = in_parts(response_ref[o])
        added = product(entering_high, high) + (product(entering_low, high) + product(entering_high, low))
        copies.append(turn_back(fixed_ref[o] + added, rows_ref, out_ref, 0, o, sent))
    for copy in copies:
        copy.wait()


def lower(fixed, response, entering, own, upper_rows):
    return pl.pallas_call(
        lower_kernel,
        out_shape=jax.ShapeDtypeStruct(OUT, jnp.float32),
        in_specs=[VMEM] * 4 + [ANY],
        out_specs=ANY,
        scratch_shapes=[pltpu.VMEM(OCTS, jnp.float32), pltpu.SemaphoreType.DMA((8,))],
        input_output_aliases={4: 0},
        name="lower",
        compiler_params=PARAMS,
    )(fixed, response, entering, own, upper_rows)


def neighbour(value, step):
    owners = range(lax.axis_size("row"))
    return lax.ppermute(value, "row", [(i, i + step) for i in owners if i + step in owners])


def local(eigvecs, reflectors):
    vectors = lax.all_to_all(pack(reflectors), "col", 0, 0, tiled=True)
    halo = neighbour(eigvecs[:SWEEPS], -1)
    return sweeps(eigvecs, halo, vectors)


def sweeps(eigvecs, halo, vectors):
    tiles = turn(eigvecs)
    after, own = rows_following(tiles, halo)
    leaving, *done = leave(tiles, vectors, after)
    entering = neighbour(leaving, 1)
    upper_rows, fixed, response = upper(*done)
    return lower(fixed, response, entering, own, upper_rows).reshape(eigvecs.shape)


def solution(mesh):
    return jax.shard_map(
        local,
        mesh=mesh,
        in_specs=(P("row", "col"), P("col", "row", None)),
        out_specs=P("row", "col"),
        check_vma=False,
    )
```

```python
import jax
import jax.numpy as jnp
from jax import lax
from jax.experimental import pallas as pl
from jax.experimental.pallas import tpu as pltpu
from jax.sharding import PartitionSpec as P

SWEEPS, BAND, HALF, LANES = 16, 64, 16, 128
TILE = (16, 128)
PARAMS = pltpu.CompilerParams(vmem_limit_bytes=8 * 2**20)


def lane_ids(shape=TILE):
    return lax.broadcasted_iota(jnp.int32, shape, len(shape) - 1)


def shear(tiles):
    slot = lane_ids(tiles[0].shape) // HALF
    for s in (1, 2, 4):
        moved = slot & s != 0
        tiles = [jnp.where(moved, tiles[(t - s) % 8], tiles[t]) for t in range(8)]
    return tiles


def swap_slots(tiles):
    tiles = shear([tiles[-t % 8] for t in range(8)])
    return shear([pltpu.roll(tiles[t], LANES - HALF * t, 1) if t else tiles[t] for t in range(8)])


def pack_kernel(reflectors_ref, copies_ref, turned_ref):
    vectors = reflectors_ref[0]
    first = lax.broadcasted_iota(jnp.int32, vectors.shape, 1) == 0
    vectors = jnp.where(first, jnp.ones_like(vectors), vectors)
    vectors = vectors * jnp.sqrt(2.0 / jnp.sum(vectors * vectors, axis=1, keepdims=True))
    padded = jnp.concatenate([vectors, jnp.zeros_like(vectors)], axis=1)
    padded = jnp.concatenate([padded] + [jnp.zeros_like(padded)] * 3, axis=0)
    turned_ref[...] = padded.T
    slot = lane_ids((8, LANES)) // HALF
    for half in range(2):
        packed = jnp.zeros((8, LANES), jnp.float32)
        for b in range(8):
            entries = turned_ref[pl.ds(b, 8, stride=8), :]
            entries = pltpu.roll(entries, (HALF * (b - half)) % LANES, 1)
            packed = jnp.where(slot == b, entries, packed)
        for sweep in range(SWEEPS):
            copies_ref[sweep, 8 * half : 8 * (half + 1), :] = packed


def pack(reflectors):
    return pl.pallas_call(
        pack_kernel,
        out_shape=jax.ShapeDtypeStruct((SWEEPS, 16, LANES), jnp.float32),
        scratch_shapes=[pltpu.VMEM((LANES, LANES), jnp.float32)],
        name="pack",
        compiler_params=PARAMS,
    )(reflectors)


def turn_kernel(rows_ref, tiles_ref, gathered_ref):
    for half in range(2):
        for o in range(8):
            for b in range(8):
                gathered_ref[half, o, HALF * b : HALF * (b + 1), :] = rows_ref[
                    pl.ds(half * HALF * BAND + 8 * o + b, HALF, stride=BAND), :
                ]
            turned = gathered_ref[half, o].T
            tiles = swap_slots([turned[HALF * g : HALF * (g + 1)] for g in range(8)])
            for b in range(8):
                tiles_ref[half, 8 * o + b] = tiles[b]


def turn(rows):
    return pl.pallas_call(
        turn_kernel,
        out_shape=jax.ShapeDtypeStruct((2, BAND) + TILE, jnp.float32),
        scratch_shapes=[pltpu.VMEM((2, 8, LANES, LANES), jnp.float32)],
        name="turn",
        compiler_params=PARAMS,
    )(rows)


def turn_back(turned, rows_ref, out_ref, half, o, sent):
    rows = turned.T
    for b in range(8):
        rows_ref[o, pl.ds(b, HALF, stride=8), :] = rows[HALF * b : HALF * (b + 1)]
    copy = pltpu.make_async_copy(
        rows_ref.at[o].reshape(HALF, 8, LANES),
        out_ref.at[pl.ds(HALF * half, HALF), pl.ds(8 * o, 8)],
        sent.at[o],
    )
    copy.start()
    return copy


def rows_after(state_ref):
    place = lane_ids() % HALF
    tile = jnp.zeros(TILE, jnp.float32)
    for i in range(SWEEPS - 1):
        tile = jnp.where(place == i, pltpu.roll(state_ref[BAND + i], (i - HALF + 1) % LANES, 1), tile)
    return tile


def spread(vectors_ref, half, sweep):
    packed = vectors_ref[sweep, 8 * half : 8 * (half + 1), :]
    return shear([pltpu.roll(packed, LANES - HALF * t, 1) if t else packed for t in range(8)])


def add_up(terms):
    while len(terms) > 1:
        terms = [sum(terms[t + 1 : t + 2], terms[t]) for t in range(0, len(terms), 2)]
    return terms[0]


def sweep_all(states, spreads, initial, entering, prepare, results, ways=2):
    tiles = [state.shape[1:] for state in states]
    heads = [lane_ids(tile) % HALF == 0 for tile in tiles]
    halves = range(len(states))

    def entry(half, sweep, i):
        at = 8 * (i % 8) + i // 8
        return jnp.broadcast_to(spreads[half][sweep, at : at + 1, :], tiles[half])

    def before(half, sweep, i):
        return initial[half](i) if sweep == SWEEPS - 1 else states[half][i]

    def add(sums, i, term):
        sums[i % ways] = term if sums[i % ways] is None else sums[i % ways] + term

    if prepare:
        for sweep in range(SWEEPS - 1, SWEEPS - 4, -1):
            prepare(sweep)
    sums = [[None] * ways for half in halves]
    for i in range(BAND):
        for half in halves:
            add(sums[half], i, entry(half, SWEEPS - 1, i) * initial[half](SWEEPS - 1 + i))
    totals = [add_up(terms) for terms in sums]
    for sweep in range(SWEEPS - 1, 0, -1):
        at = sweep + BAND - 1
        lasts = [before(half, sweep, at) - entry(half, sweep, BAND - 1) * totals[half] for half in halves]
        firsts = [
            jnp.where(heads[half], rows, pltpu.roll(lasts[half], 1, 1))
            for half, rows in enumerate(entering(sweep, lasts))
        ]
        for half in halves:
            states[half][at] = lasts[half]
            states[half][sweep - 1] = firsts[half]
        if prepare and sweep >= 3:
            prepare(sweep - 3)
        sums = [[None] * ways for half in halves]
        for i in range(BAND - 1):
            for half in halves:
                row = before(half, sweep, sweep + i) - entry(half, sweep, i) * totals[half]
                states[half][sweep + i] = row
                add(sums[half], i, entry(half, sweep - 1, i + 1) * row)
        totals = [add_up(sums[half]) + entry(half, sweep - 1, 0) * firsts[half] for half in halves]
    for i in range(BAND):
        for half in halves:
            results[half][i] = states[half][i] - entry(half, 0, i) * totals[half]


def rows_of(tiles_ref, after_ref, half):
    return lambda i: tiles_ref[half, i] if i < BAND else after_ref[half, i - BAND]


def after_kernel(tiles_ref, halo_ref, after_ref, own_ref, gathered_ref):
    place, own_rows = lane_ids() % HALF, jnp.zeros(TILE, jnp.float32)
    for i in range(SWEEPS - 1):
        own_rows = jnp.where(place == i, pltpu.roll(tiles_ref[0, i], i, 1) if i else tiles_ref[0, 0], own_rows)
    own_ref[...] = own_rows
    last = lane_ids() % HALF == HALF - 1
    gathered_ref[...] = jnp.zeros_like(gathered_ref)
    gathered_ref[:HALF, :] = halo_ref[...]
    turned = gathered_ref[...].T
    slot = lane_ids() // HALF
    halo = turned[:HALF]
    for g in range(1, 8):
        halo = jnp.where(slot == g, pltpu.roll(turned[HALF * g : HALF * (g + 1)], HALF * g, 1), halo)
    for i in range(SWEEPS - 1):
        own = [pltpu.roll(tiles_ref[half, i], LANES - 1, 1) for half in range(2)]
        after_ref[0, i] = jnp.where(last, pltpu.roll(tiles_ref[1, i], HALF - 1, 1), own[0])
        after_ref[1, i] = jnp.where(last, pltpu.roll(halo, HALF - 1 - i, 1), own[1])


def rows_following(tiles, halo):
    return pl.pallas_call(
        after_kernel,
        out_shape=(
            jax.ShapeDtypeStruct((2, SWEEPS - 1) + TILE, jnp.float32),
            jax.ShapeDtypeStruct(TILE, jnp.float32),
        ),
        scratch_shapes=[pltpu.VMEM((LANES, LANES), jnp.float32)],
        name="after",
        compiler_params=PARAMS,
    )(tiles, halo)


def leave_kernel(
    tiles_ref, vectors_ref, after_ref,
    leaving_ref, lower_done_ref, upper_done_ref, spread_done_ref,
    lower_ref, upper_ref, lower_spread_ref, upper_spread_ref,
):
    zeros = jnp.zeros(TILE, jnp.float32)
    rows = [rows_of(tiles_ref, after_ref, half) for half in range(2)]
    spreads = lower_spread_ref, upper_spread_ref

    def prepare(sweep):
        for half in range(2):
            for b, tile in enumerate(spread(vectors_ref, half, sweep)):
                spreads[half][sweep, 8 * b : 8 * (b + 1), :] = tile
                if half == 0:
                    spread_done_ref[sweep, 8 * b : 8 * (b + 1), :] = tile

    for sweep in range(SWEEPS - 1, -1, -1):
        prepare(sweep)
    sweep_all(
        (lower_ref, upper_ref),
        spreads,
        rows,
        lambda sweep, lasts: (zeros, pltpu.roll(lasts[0], LANES - HALF + 1, 1)),
        None,
        (lower_done_ref, upper_done_ref),
    )
    leaving_ref[...] = rows_after(upper_ref)


STATE, WIDE, SPREAD = (BAND + SWEEPS,) + TILE, (BAND + SWEEPS, 24, LANES), (SWEEPS, BAND, LANES)
OCTS = (8, LANES, LANES)
OUT = (2 * HALF, BAND, LANES)
VMEM, ANY = pl.BlockSpec(memory_space=pltpu.VMEM), pl.BlockSpec(memory_space=pl.ANY)


def leave(tiles, vectors, after):
    shapes = TILE, (BAND,) + TILE, (BAND,) + TILE, SPREAD
    return pl.pallas_call(
        leave_kernel,
        out_shape=tuple(jax.ShapeDtypeStruct(shape, jnp.float32) for shape in shapes),
        scratch_shapes=[pltpu.VMEM(shape, jnp.float32) for shape in (STATE, STATE, SPREAD, SPREAD)],
        name="leave",
        compiler_params=PARAMS,
    )(tiles, vectors, after)


def unit_sweeps(spread_ref, unit_ref, gaps):
    tile = (8, LANES)
    row, lane = lax.broadcasted_iota(jnp.int32, tile, 0), lane_ids(tile)
    zeros = jnp.zeros(tile, jnp.float32)

    def entering(sweep, lasts):
        i = sweep - 1
        gaps(sweep)
        return (jnp.where(jnp.logical_and(row == i % 8, lane // HALF % 2 == i // 8), 1.0, 0.0),)

    sweep_all((unit_ref,), (spread_ref,), (lambda i: zeros,), entering, None, (unit_ref,), 4)


def upper_kernel(lower_ref, upper_ref, spread_ref, out_ref, fixed_ref, response_ref, rows_ref, sent, unit_ref):
    copies = []

    def gaps(sweep):
        if sweep % 2:
            o = 7 - sweep // 2
            turned = jnp.concatenate(swap_slots([upper_ref[8 * o + b] for b in range(8)]), axis=0)
            copies.append(turn_back(turned, rows_ref, out_ref, 1, o, sent))

    unit_sweeps(spread_ref, unit_ref, gaps)
    slot = lane_ids((8, LANES)) // HALF
    for o in range(8):
        fixed_ref[o] = jnp.concatenate(swap_slots([lower_ref[8 * o + b] for b in range(8)]), axis=0)
        first, second = None, None
        for b in range(8):
            one = unit_ref[8 * o + b]
            parts = one, pltpu.roll(one, HALF, 1)
            first = parts[0] if first is None else jnp.where(slot == b, parts[b % 2], first)
            second = parts[1] if second is None else jnp.where(slot == b, parts[1 - b % 2], second)
        response_ref[o, :8, :] = first
        response_ref[o, 8:, :] = second
    for copy in copies:
        copy.wait()


def upper(*operands):
    return pl.pallas_call(
        upper_kernel,
        out_shape=tuple(jax.ShapeDtypeStruct(shape, jnp.float32) for shape in (OUT, OCTS, (8,) + TILE)),
        out_specs=(ANY, VMEM, VMEM),
        scratch_shapes=[
            pltpu.VMEM(OCTS, jnp.float32),
            pltpu.SemaphoreType.DMA((8,)),
            pltpu.VMEM((BAND + SWEEPS, 8, LANES), jnp.float32),
        ],
        name="upper",
        compiler_params=PARAMS,
    )(*operands)


def in_parts(values):
    high = values.astype(jnp.bfloat16)
    return high, (values - high.astype(jnp.float32)).astype(jnp.bfloat16)


def product(a, b):
    return jnp.dot(a, b, preferred_element_type=jnp.float32)


def lower_kernel(fixed_ref, response_ref, entering_ref, own_ref, upper_ref, out_ref, rows_ref, sent):
    tile = jnp.where(lax.axis_index("row") == 0, own_ref[...], entering_ref[...])
    entering = jnp.concatenate(
        [tile] + [pltpu.roll(tile, LANES - HALF * g, 1) for g in range(1, 8)], axis=0
    )[:, :HALF]
    entering_high, entering_low = in_parts(entering)
    copies = []
    for o in range(8):
        high, low = in_parts(response_ref[o])
        added = product(entering_high, high) + (product(entering_low, high) + product(entering_high, low))
        copies.append(turn_back(fixed_ref[o] + added, rows_ref, out_ref, 0, o, sent))
    for copy in copies:
        copy.wait()


def lower(fixed, response, entering, own, upper_rows):
    return pl.pallas_call(
        lower_kernel,
        out_shape=jax.ShapeDtypeStruct(OUT, jnp.float32),
        in_specs=[VMEM] * 4 + [ANY],
        out_specs=ANY,
        scratch_shapes=[pltpu.VMEM(OCTS, jnp.float32), pltpu.SemaphoreType.DMA((8,))],
        input_output_aliases={4: 0},
        name="lower",
        compiler_params=PARAMS,
    )(fixed, response, entering, own, upper_rows)


def neighbour(value, step):
    owners = range(lax.axis_size("row"))
    return lax.ppermute(value, "row", [(i, i + step) for i in owners if i + step in owners])


def local(eigvecs, reflectors):
    vectors = lax.all_to_all(pack(reflectors), "col", 0, 0, tiled=True)
    halo = neighbour(eigvecs[:SWEEPS], -1)
    return sweeps(eigvecs, halo, vectors)


def sweeps(eigvecs, halo, vectors):
    tiles = turn(eigvecs)
    after, own = rows_following(tiles, halo)
    leaving, *done = leave(tiles, vectors, after)
    entering = neighbour(leaving, 1)
    upper_rows, fixed, response = upper(*done)
    return lower(fixed, response, entering, own, upper_rows).reshape(eigvecs.shape)


def solution(mesh):
    return jax.shard_map(
        local,
        mesh=mesh,
        in_specs=(P("row", "col"), P("col", "row", None)),
        out_specs=P("row", "col"),
        check_vma=False,
    )
```
